32 devices in a mesh: az: 8 (over z, y), rg: 4 (over x, core).
Axes of the slice: x: 2, y: 2, z: 4, core: 2. Of those that a mesh axis runs over, the one named last changes fastest.
Arguments:
- echoes: bfloat16 [2, 8192, 16384], P(None, 'rg', 'az'), may hold values from -6 to 6
- replica: bfloat16 [2, 2048], replicated, may hold values from -0.125 to 0.125
- shifts: int32 [512, 8], replicated, may hold values from 0 to 16, as said below
- tap_counts: int32 [512], replicated, may hold values from 1 to 8
- interp_weights: float32 [512, 8], replicated, may hold values from -2 to 2
- fm_rates: float32 [512], replicated, may hold values from 50 to 1000
Outputs:
- focused_image: float32 [2, 8192, 16384], P(None, ('rg', 'az'))
The draws below stay inside these ranges and needn't reach their ends.
Inputs may be any that keep to these rules, and one draw needn't show every extreme that they name: `shifts`: in some range band and Doppler block the shift is 16 while that band uses all 8 taps.
All inputs are finite; a program needn't handle non-finite values.
Results may differ from the reference program's by a relative error of at most 0.0029.
Values may be sent and summed in bfloat16 or wider, within the bound.
A program may use at most 320 MiB of HBM per device.

```python
import math
import jax
import jax.numpy as jnp
from jax import lax

AZIMUTH = 16384
RANGE_BINS = 8192
CHIRP_TAPS = 2048
INTERP_TAPS = 8
MAX_SHIFT = 16
BAND_BINS = 16
DOPPLER_BLOCKS = 8
BAND_COUNT = 512
RIM_BINS = 23


def migration_tables(key):
    shift_key = jax.random.fold_in(key, 101)
    count_key = jax.random.fold_in(key, 102)
    band_key = jax.random.fold_in(key, 103)
    block_key = jax.random.fold_in(key, 104)
    shifts = jax.random.randint(shift_key, (BAND_COUNT, DOPPLER_BLOCKS), 0, MAX_SHIFT + 1, dtype=jnp.int32)
    counts = jax.random.randint(count_key, (BAND_COUNT,), 1, INTERP_TAPS + 1, dtype=jnp.int32)
    chosen_band = jax.random.randint(band_key, (), 0, BAND_COUNT, dtype=jnp.int32)
    chosen_block = jax.random.randint(block_key, (), 0, DOPPLER_BLOCKS, dtype=jnp.int32)
    shifts = shifts.at[chosen_band, chosen_block].set(MAX_SHIFT)
    counts = counts.at[chosen_band].set(INTERP_TAPS)
    return (shifts, counts)


def draw_shifts(key, part):
    return migration_tables(key)[0]


def draw_tap_counts(key, part):
    return migration_tables(key)[1]


def block_scale(own_key, dims, cuts, smallest, largest):
    def one(axis_at, blocks):
        draws = jax.random.uniform(jax.random.fold_in(jax.random.fold_in(own_key, 6), axis_at), (blocks,), jnp.float32, smallest / len(cuts), largest / len(cuts))
        return jnp.repeat(jnp.exp(draws), dims[axis_at] // blocks).reshape((-1,) + (1,) * (len(dims) - axis_at - 1))

    loudness = one(*cuts[0])
    for cut in cuts[1:]:
        loudness = loudness * one(*cut)
    return loudness


def normal_values(own_key, dims, width, reach, cuts=(), kind=jnp.bfloat16):
    loudness = block_scale(own_key, dims, cuts, -0.22, 0.18) if cuts else 1.0
    drawn = jax.random.normal(own_key, dims, jnp.float32) * width * loudness
    return jnp.minimum(jnp.maximum(drawn, -reach), reach).astype(kind)


def setup_inputs(seed: int = 0) -> dict:
    splits = jax.random.split(jax.random.key(seed), 7)
    return {
        "echoes": normal_values(splits[0], (2, RANGE_BINS, AZIMUTH), 1.0, 6.0, ((1, 4), (2, 8))),
        "replica": normal_values(splits[1], (2, CHIRP_TAPS), CHIRP_TAPS ** -0.5, 0.125),
        "shifts": draw_shifts(jax.random.fold_in(splits[6], 71), 0),
        "tap_counts": draw_tap_counts(jax.random.fold_in(splits[6], 71), 0),
        "interp_weights": normal_values(splits[4], (BAND_COUNT, INTERP_TAPS), 0.35, 2.0, (), jnp.float32),
        "fm_rates": jnp.clip(jnp.exp(jax.random.uniform(splits[5], (BAND_COUNT,), jnp.float32, math.log(50.0), math.log(1000.0))), 50.0, 1000.0),
    }


def reference(echoes, replica, shifts, tap_counts, interp_weights, fm_rates):
    padded_len = RANGE_BINS + CHIRP_TAPS
    pulse = lax.complex(replica[0].astype(jnp.float32), replica[1].astype(jnp.float32))
    kernel = jnp.conj(jnp.fft.fft(pulse, n=padded_len))
    block_lines = min(512, AZIMUTH)
    line_blocks = AZIMUTH // block_lines
    grouped = echoes.reshape(2, RANGE_BINS, line_blocks, block_lines).transpose(2, 0, 1, 3)

    def compress(line_group):
        signal = lax.complex(line_group[0].astype(jnp.float32), line_group[1].astype(jnp.float32))
        spectra = jnp.fft.fft(signal, n=padded_len, axis=0)
        correlated = jnp.fft.ifft(spectra * kernel[:, None], axis=0)[:RANGE_BINS]
        return jnp.stack([jnp.real(correlated), jnp.imag(correlated)]).astype(jnp.bfloat16)

    pieces = lax.map(compress, grouped)
    compressed = pieces.transpose(1, 2, 0, 3).reshape(2, RANGE_BINS, AZIMUTH)

    def transform(row_group):
        return jnp.fft.fft(lax.complex(row_group[0].astype(jnp.float32), row_group[1].astype(jnp.float32)), axis=-1)

    by_band = compressed.reshape(2, BAND_COUNT, BAND_BINS, AZIMUTH).transpose(1, 0, 2, 3)
    spectrum = lax.map(transform, by_band).reshape(RANGE_BINS, AZIMUTH)
    padded = jnp.concatenate([spectrum, jnp.zeros((RIM_BINS, AZIMUTH), spectrum.dtype)], axis=0)
    col_width = AZIMUTH // DOPPLER_BLOCKS
    doppler = jnp.arange(AZIMUTH, dtype=jnp.int32)
    signed = jnp.where(doppler < AZIMUTH // 2, doppler, doppler - AZIMUTH).astype(jnp.float32) / AZIMUTH
    squared = signed * signed

    def focus(band_idx):
        columns = []
        for dop_block in range(DOPPLER_BLOCKS):
            summed = jnp.zeros((BAND_BINS, col_width), spectrum.dtype)
            for tap_idx in range(INTERP_TAPS):
                row_start = (band_idx * BAND_BINS + shifts[band_idx, dop_block] + tap_idx).astype(jnp.int32)
                segment = lax.dynamic_slice(padded, (row_start, jnp.int32(dop_block * col_width)), (BAND_BINS, col_width))
                weight = jnp.where(tap_idx < tap_counts[band_idx], interp_weights[band_idx, tap_idx], 0.0)
                summed = summed + weight * segment
            columns.append(summed)
        migrated = jnp.concatenate(columns, axis=1)
        phases = math.pi * fm_rates[band_idx] * squared
        focused = migrated * lax.complex(jnp.cos(phases), -jnp.sin(phases))
        result = jnp.fft.ifft(focused, axis=-1)
        return jnp.stack([jnp.real(result), jnp.imag(result)]).astype(jnp.float32)

    images = lax.map(focus, jnp.arange(BAND_COUNT, dtype=jnp.int32))
    return images.transpose(1, 0, 2, 3).reshape(2, RANGE_BINS, AZIMUTH)
```

```python
import functools
import math

import jax
import jax.numpy as jnp
import numpy as np
from jax import lax
from jax.experimental import pallas as pl
from jax.experimental.pallas import tpu as pltpu
from jax.sharding import PartitionSpec as P

SIDE = 128
INTERP_TAPS = 8
MAX_SHIFT = 16
BAND_BINS = 16
DOPPLER_BLOCKS = 8
COMPRESS_ROWS = 256
RIM_ROWS = 32
VMEM = 56 * 1024 * 1024


def transform_tables():
    k = np.arange(SIDE)
    angle = 2.0 * np.pi * ((k[:, None] * k[None, :]) % SIDE) / SIDE
    c, s = np.cos(angle), np.sin(angle)
    forward = np.block([[c, s], [-s, c]])
    inverse = np.block([[c, -s], [s, c]])
    twist = 2.0 * np.pi * (k[:, None] * k[None, :]) / (SIDE * SIDE)
    return forward, inverse, np.cos(twist), np.sin(twist)


def split_const(matrix):
    high = jnp.asarray(matrix, jnp.float32).astype(jnp.bfloat16)
    low_np = np.asarray(matrix, np.float64) - np.asarray(
        np.asarray(matrix, np.float32).astype(jnp.bfloat16), np.float64
    )
    return jnp.stack([high, jnp.asarray(low_np, jnp.float32).astype(jnp.bfloat16)])


def split_data(value):
    high = value.astype(jnp.bfloat16)
    return high, (value - high.astype(jnp.float32)).astype(jnp.bfloat16)


NN = (((1,), (0,)), ((), ()))
NT = (((1,), (1,)), ((), ()))
MESH = pl.DeviceIdType.MESH


def mm(a, b, dims):
    return lax.dot_general(a, b, dims, preferred_element_type=jnp.float32)


def mm2(table, data, dims):
    return mm(table[0], data, dims) + mm(table[1], data, dims)


def mm3(table, value, dims):
    high, low = split_data(value)
    return mm(table[0], high, dims) + (mm(table[1], high, dims) + mm(table[0], low, dims))


def exchange_kernel(
    width, block_rows, w_ref, echoes_ref, turned_ref,
    window, staging, load_sem, rim_send, rim_recv, out_send, out_recv, halo_send
):
    az_count, rg_count = lax.axis_size("az"), lax.axis_size("rg")
    a, g = lax.axis_index("az"), lax.axis_index("rg")
    last = az_count - 1
    rows, lines = echoes_ref.shape[1], echoes_ref.shape[2]
    taps = window.shape[1] - rows
    span = w_ref.shape[2]
    local_rows = rows // az_count
    chunks = lines // width
    has_before, has_after = g > 0, g < rg_count - 1
    before = lax.rem(g + rg_count - 1, rg_count)
    after = lax.rem(g + 1, rg_count)

    def columns(c):
        return pl.ds(pl.multiple_of(c * width, width), width)

    def own_load(c):
        return pltpu.make_async_copy(
            echoes_ref.at[:, :, columns(c)],
            window.at[:, pl.ds(0, rows), columns(c)],
            load_sem.at[c],
        )

    def rim_copy(c):
        return pltpu.make_async_remote_copy(
            src_ref=echoes_ref.at[:, pl.ds(0, taps), columns(c)],
            dst_ref=window.at[:, pl.ds(rows, taps), columns(c)],
            send_sem=rim_send.at[c],
            recv_sem=rim_recv.at[c],
            device_id=(a, before),
            device_id_type=MESH,
        )

    def start_load(c, _):
        own_load(c).start()
        return 0

    lax.fori_loop(0, chunks, start_load, 0)

    barrier = pltpu.get_barrier_semaphore()

    def greet(az_at, rg_at):
        pl.semaphore_signal(barrier, inc=1, device_id=(az_at, rg_at), device_id_type=MESH)

    def greet_peer(d, _):
        greet(lax.rem(a + d, az_count), g)
        return 0

    lax.fori_loop(1, az_count, greet_peer, 0)

    @pl.when(has_before)
    def _():
        greet(a, before)

    @pl.when(has_after)
    def _():
        greet(a, after)

    @pl.when(has_before & (a != last))
    def _():
        greet(last, before)

    @pl.when(has_after & (a == last))
    def _():
        def greet_halo(b, _):
            greet(b, after)
            return 0

        lax.fori_loop(0, last, greet_halo, 0)

    one = lambda flag: jnp.where(flag, 1, 0)
    pl.semaphore_wait(
        barrier,
        last
        + one(has_before)
        + one(has_after)
        + one(has_before & (a != last))
        + last * one(has_after & (a == last)),
    )

    upfront = jnp.where(lax.rem(g, 2) == 1, chunks, min(2, chunks))

    @pl.when(has_before)
    def _():
        def start_rim(c, _):
            rim_copy(c).start()
            return 0

        lax.fori_loop(0, upfront, start_rim, 0)

    @pl.when(jnp.logical_not(has_after))
    def _():
        def clear(i, _):
            at = pl.ds(pl.multiple_of(rows + i * 128, 128), 128)
            window[:, at, :] = jnp.zeros((2, 128, lines), window.dtype)
            return 0

        lax.fori_loop(0, taps // 128, clear, 0)

        @pl.when(a == last)
        def _():
            staging[:, rows:, :] = jnp.zeros((2, RIM_ROWS, lines), staging.dtype)

            def clear_halo(b, _):
                pltpu.make_async_copy(
                    staging.at[:, pl.ds(rows, RIM_ROWS), :],
                    turned_ref.at[b, :, pl.ds(local_rows, RIM_ROWS), :],
                    out_recv.at[b],
                ).start()
                return 0

            lax.fori_loop(0, az_count, clear_halo, 0)

    def block_copy(b, height, cols):
        return pltpu.make_async_remote_copy(
            src_ref=staging.at[:, pl.ds(pl.multiple_of(b * local_rows, local_rows), height), cols],
            dst_ref=turned_ref.at[a, :, pl.ds(0, height), cols],
            send_sem=out_send.at[b],
            recv_sem=out_recv.at[a],
            device_id=(b, g),
            device_id_type=MESH,
        )

    def own_copy(height, cols):
        return pltpu.make_async_copy(
            staging.at[:, pl.ds(pl.multiple_of(a * local_rows, local_rows), height), cols],
            turned_ref.at[a, :, pl.ds(0, height), cols],
            out_recv.at[a],
        )

    def halo_copy(cols):
        return pltpu.make_async_remote_copy(
            src_ref=staging.at[:, pl.ds(0, RIM_ROWS), cols],
            dst_ref=turned_ref.at[a, :, pl.ds(local_rows, RIM_ROWS), cols],
            send_sem=halo_send.at[0],
            recv_sem=out_recv.at[a],
            device_id=(last, before),
            device_id_type=MESH,
        )

    tall = local_rows + RIM_ROWS

    def chunk(c, _):
        cols = columns(c)
        own_load(c).wait()

        @pl.when(has_after)
        def _():
            rim_copy(c).wait_recv()

        def block(i, _):
            start = pl.multiple_of(i * block_rows, block_rows)
            total = mm(w_ref[0], window[0, pl.ds(start, span), cols], NN)
            total = total + mm(w_ref[1], window[1, pl.ds(start, span), cols], NN)
            total = total.astype(jnp.bfloat16)
            staging[0, pl.ds(start, block_rows), cols] = total[:block_rows]
            staging[1, pl.ds(start, block_rows), cols] = total[block_rows:]
            return 0

        lax.fori_loop(0, rows // block_rows, block, 0)

        def send(d, _):
            b = lax.rem(a + d, az_count)

            @pl.when(b == last)
            def _():
                block_copy(b, local_rows, cols).start()

            @pl.when(b != last)
            def _():
                block_copy(b, tall, cols).start()

            return 0

        lax.fori_loop(1, az_count, send, 0)

        @pl.when(a == last)
        def _():
            own_copy(local_rows, cols).start()

        @pl.when(a != last)
        def _():
            own_copy(tall, cols).start()

        @pl.when(has_before)
        def _():
            halo_copy(cols).start()
            rim_copy(c).wait_send()

            @pl.when(c + upfront < chunks)
            def _():
                rim_copy(c + upfront).start()

        return 0

    lax.fori_loop(0, chunks, chunk, 0)

    every = pl.ds(0, lines)

    def finish_send(d, _):
        b = lax.rem(a + d, az_count)

        @pl.when(b == last)
        def _():
            block_copy(b, local_rows, every).wait_send()

        @pl.when(b != last)
        def _():
            block_copy(b, tall, every).wait_send()

        return 0

    lax.fori_loop(1, az_count, finish_send, 0)

    @pl.when(has_before)
    def _():
        halo_copy(every).wait_send()

    def finish_receive(b, _):
        pltpu.make_async_copy(turned_ref.at[b], turned_ref.at[b], out_recv.at[b]).wait()
        return 0

    lax.fori_loop(0, az_count, finish_receive, 0)


def exchange(weights, echoes, az_count):
    rows, lines = echoes.shape[1], echoes.shape[2]
    span = weights.shape[2]
    block_rows = weights.shape[1] // 2
    taps = span - block_rows
    width = math.gcd(256, lines)
    chunks = lines // width
    local_rows = rows // az_count
    return pl.pallas_call(
        functools.partial(exchange_kernel, width, block_rows),
        out_shape=jax.ShapeDtypeStruct(
            (az_count, 2, local_rows + RIM_ROWS, lines), jnp.bfloat16
        ),
        in_specs=[
            pl.BlockSpec(memory_space=pltpu.VMEM),
            pl.BlockSpec(memory_space=pl.ANY),
        ],
        out_specs=pl.BlockSpec(memory_space=pl.ANY),
        scratch_shapes=[
            pltpu.VMEM((2, rows + taps, lines), jnp.bfloat16),
            pltpu.VMEM((2, rows + RIM_ROWS, lines), jnp.bfloat16),
            pltpu.SemaphoreType.DMA((chunks,)),
            pltpu.SemaphoreType.DMA((chunks,)),
            pltpu.SemaphoreType.DMA((chunks,)),
            pltpu.SemaphoreType.DMA((az_count,)),
            pltpu.SemaphoreType.DMA((az_count,)),
            pltpu.SemaphoreType.DMA((1,)),
        ],
        compiler_params=pltpu.CompilerParams(
            vmem_limit_bytes=60 * 1024 * 1024, collective_id=0, has_side_effects=True
        ),
        cost_estimate=pl.CostEstimate(
            flops=8 * rows * span * lines,
            bytes_accessed=4 * lines * (4 * rows + taps),
            transcendentals=0,
        ),
        name="exchange",
    )(weights, echoes)


def compress_weights(replica, block_rows):
    taps = replica.shape[1]
    span = taps + block_rows

    def banded(vector):
        cycled = jnp.concatenate([vector, jnp.zeros((span + 1 - taps,), vector.dtype)])
        return jnp.tile(cycled, block_rows)[: block_rows * span].reshape(block_rows, span)

    real_rows = banded(replica[0])
    imag_rows = banded(replica[1])
    return jnp.stack(
        [
            jnp.concatenate([real_rows, -imag_rows], axis=0),
            jnp.concatenate([imag_rows, real_rows], axis=0),
        ]
    )


def forward_kernel(table_ref, cos_ref, sin_ref, in_ref, *rest):
    out_ref, data = rest[-2], rest[-1]
    az_count, _, rows, lines = in_ref.shape
    per = lines // SIDE
    for source in range(az_count):
        for c in range(2):
            piece = in_ref[source, c].astype(jnp.float32)
            data[:, c * SIDE + source * per : c * SIDE + (source + 1) * per, :] = piece.reshape(
                rows, per, SIDE
            )

    def pair(i, _):
        both = jnp.concatenate([data[2 * i], data[2 * i + 1]], axis=1).astype(jnp.bfloat16)
        first = mm2(table_ref, both, NN)
        cosine, sine = cos_ref[...], sin_ref[...]
        turned = []
        for k in range(2):
            real = first[:SIDE, k * SIDE : (k + 1) * SIDE]
            imag = first[SIDE:, k * SIDE : (k + 1) * SIDE]
            turned.append(
                jnp.concatenate(
                    [real * cosine + imag * sine, imag * cosine - real * sine], axis=1
                )
            )
        second = mm3(table_ref, jnp.concatenate(turned, axis=0), NT)
        for k in range(2):
            out_ref[0, 2 * i + k] = second[:SIDE, k * SIDE : (k + 1) * SIDE]
            out_ref[1, 2 * i + k] = second[SIDE:, k * SIDE : (k + 1) * SIDE]
        return 0

    lax.fori_loop(0, rows // 2, pair, 0, unroll=2)


def forward(tables, lines_in, held, first_block, total_rows):
    table, cosine, sine = tables
    az_count, _, rows, lines = lines_in.shape
    whole2 = lambda i: (0, 0)
    in_specs = [
        pl.BlockSpec(table.shape, lambda i: (0, 0, 0)),
        pl.BlockSpec((SIDE, SIDE), whole2),
        pl.BlockSpec((SIDE, SIDE), whole2),
        pl.BlockSpec((az_count, 2, BAND_BINS, lines), lambda i: (0, 0, i, 0)),
    ]
    operands = [table, cosine, sine, lines_in]
    aliases = {}
    if held is not None:
        in_specs.append(pl.BlockSpec(memory_space=pl.ANY))
        operands.append(held)
        aliases = {4: 0}
    return pl.pallas_call(
        forward_kernel,
        out_shape=jax.ShapeDtypeStruct((2, total_rows, SIDE, SIDE), jnp.float32),
        grid=(rows // BAND_BINS,),
        in_specs=in_specs,
        out_specs=pl.BlockSpec((2, BAND_BINS, SIDE, SIDE), lambda i: (0, first_block + i, 0, 0)),
        scratch_shapes=[pltpu.VMEM((BAND_BINS, 2 * SIDE, SIDE), jnp.float32)],
        input_output_aliases=aliases,
        compiler_params=pltpu.CompilerParams(vmem_limit_bytes=VMEM),
        cost_estimate=pl.CostEstimate(
            flops=rows * 5 * 2 * 2 * SIDE * 2 * SIDE * SIDE * 2,
            bytes_accessed=rows * SIDE * SIDE * 12,
            transcendentals=0,
        ),
        name=f"forward_at_{first_block}",
    )(*operands)


def focus_kernel(
    shift_ref, weight_ref, table_ref, cos_ref, sin_ref, pcos_ref, psin_ref,
    spec0, spec1, spec2, out_ref, window, moved, image
):
    band = pl.program_id(0)
    for k, ref in enumerate((spec0, spec1, spec2)):
        keep = BAND_BINS if k < 2 else INTERP_TAPS
        window[:, k * BAND_BINS : k * BAND_BINS + keep] = ref[:, :keep]
    deep = SIDE // DOPPLER_BLOCKS
    taps = [weight_ref[band, t] for t in range(INTERP_TAPS)]

    def block(d, _):
        shift = shift_ref[band, d]
        spot = pl.ds(pl.multiple_of(d * deep, deep), deep)
        pcos, psin = pcos_ref[0, spot, :], psin_ref[0, spot, :]
        sums = []
        for half in range(2):
            rows = BAND_BINS // 2
            parts = []
            for c in range(2):
                total = taps[0] * window[c, pl.ds(shift + half * rows, rows), spot, :]
                for t in range(1, INTERP_TAPS):
                    total = total + taps[t] * window[c, pl.ds(shift + half * rows + t, rows), spot, :]
                parts.append(total)
            real, imag = parts
            put = slice(half * rows, (half + 1) * rows)
            moved[put, spot, :] = real * pcos + imag * psin
            low = pl.ds(pl.multiple_of(SIDE + d * deep, deep), deep)
            moved[put, low, :] = imag * pcos - real * psin
        return 0

    lax.fori_loop(0, DOPPLER_BLOCKS, block, 0)

    def pair(i, _):
        both = jnp.concatenate([moved[2 * i], moved[2 * i + 1]], axis=1)
        first = mm3(table_ref, both, NN)
        cosine, sine = cos_ref[...], sin_ref[...]
        turned = []
        for k in range(2):
            real = first[:SIDE, k * SIDE : (k + 1) * SIDE]
            imag = first[SIDE:, k * SIDE : (k + 1) * SIDE]
            turned.append(
                jnp.concatenate(
                    [real * cosine - imag * sine, imag * cosine + real * sine], axis=1
                )
            )
        second = mm2(table_ref, jnp.concatenate(turned, axis=0).astype(jnp.bfloat16), NT)
        second = second * (1.0 / (SIDE * SIDE))
        for k in range(2):
            image[2 * i + k] = second[:, k * SIDE : (k + 1) * SIDE]
        return 0

    lax.fori_loop(0, BAND_BINS // 2, pair, 0, unroll=2)
    group = 16
    for c in range(2):
        for g in range(SIDE // group):
            piece = image[:, c * SIDE + g * group : c * SIDE + (g + 1) * group, :]
            out_ref[c, :, g * group * SIDE : (g + 1) * group * SIDE] = piece.reshape(
                BAND_BINS, group * SIDE
            )


def focus(shifts, weights, tables, pcos, psin, spectrum, local_rows):
    table, cosine, sine = tables
    whole2 = lambda i, *_: (0, 0)

    def part(k):
        return pl.BlockSpec((2, BAND_BINS, SIDE, SIDE), lambda i, *_: (0, i + k, 0, 0))

    phase_spec = pl.BlockSpec((1, SIDE, SIDE), lambda i, *_: (i, 0, 0))
    return pl.pallas_call(
        focus_kernel,
        out_shape=jax.ShapeDtypeStruct((2, local_rows, SIDE * SIDE), jnp.float32),
        grid_spec=pltpu.PrefetchScalarGridSpec(
            num_scalar_prefetch=2,
            grid=(local_rows // BAND_BINS,),
            in_specs=[
                pl.BlockSpec(table.shape, lambda i, *_: (0, 0, 0)),
                pl.BlockSpec((SIDE, SIDE), whole2),
                pl.BlockSpec((SIDE, SIDE), whole2),
                phase_spec,
                phase_spec,
                part(0),
                part(1),
                part(2),
            ],
            out_specs=pl.BlockSpec((2, BAND_BINS, SIDE * SIDE), lambda i, *_: (0, i, 0)),
            scratch_shapes=[
                pltpu.VMEM((2, 2 * BAND_BINS + INTERP_TAPS, SIDE, SIDE), jnp.float32),
                pltpu.VMEM((BAND_BINS, 2 * SIDE, SIDE), jnp.float32),
                pltpu.VMEM((BAND_BINS, 2 * SIDE, SIDE), jnp.float32),
            ],
        ),
        compiler_params=pltpu.CompilerParams(vmem_limit_bytes=VMEM),
        name="focus",
    )(shifts, weights, table, cosine, sine, pcos, psin, spectrum, spectrum, spectrum)


def per_device(echoes, replica, shifts, tap_counts, interp_weights, fm_rates):
    range_dev = echoes.shape[1]
    az_count = lax.axis_size("az")
    rg_count = lax.axis_size("rg")
    local_rows = range_dev // az_count
    block_rows = COMPRESS_ROWS
    bands_here = local_rows // BAND_BINS
    az_pos = lax.axis_index("az")
    rg_pos = lax.axis_index("rg")

    weights = compress_weights(replica, block_rows)
    forward_m, inverse_m, twist_cos, twist_sin = transform_tables()
    cosine = jnp.asarray(twist_cos, jnp.float32)
    sine = jnp.asarray(twist_sin, jnp.float32)
    forward_tables = (split_const(forward_m), cosine, sine)
    inverse_tables = (split_const(inverse_m), cosine, sine)

    band_first = (rg_pos * range_dev + az_pos * local_rows) // BAND_BINS
    band_shift = lax.dynamic_slice_in_dim(shifts, band_first, bands_here)
    band_taps = lax.dynamic_slice_in_dim(tap_counts, band_first, bands_here)
    band_weight = lax.dynamic_slice_in_dim(interp_weights, band_first, bands_here)
    tap_index = lax.broadcasted_iota(jnp.int32, (bands_here, INTERP_TAPS), 1)
    live_weight = jnp.where(tap_index < band_taps[:, None], band_weight, 0.0)
    band_rate = lax.dynamic_slice_in_dim(fm_rates, band_first, bands_here)
    total_lines = SIDE * SIDE
    doppler = SIDE * lax.broadcasted_iota(jnp.int32, (SIDE, SIDE), 0) + lax.broadcasted_iota(
        jnp.int32, (SIDE, SIDE), 1
    )
    signed = (
        jnp.where(doppler < total_lines // 2, doppler, doppler - total_lines).astype(jnp.float32)
        / total_lines
    )
    phases = math.pi * band_rate[:, None, None] * (signed * signed)[None]
    pcos = jnp.cos(phases)
    psin = jnp.sin(phases)

    turned = exchange(weights, echoes, az_count)
    total_rows = local_rows + RIM_ROWS
    spectrum = forward(forward_tables, turned, None, 0, total_rows)
    return focus(band_shift, live_weight, inverse_tables, pcos, psin, spectrum, local_rows)


def solution(mesh):
    return jax.shard_map(
        per_device,
        mesh=mesh,
        in_specs=(P(None, "rg", "az"), P(), P(), P(), P(), P()),
        out_specs=P(None, ("rg", "az"), None),
        check_vma=False,
    )
```

```python
import functools
import math

import jax
import jax.numpy as jnp
import numpy as np
from jax import lax
from jax.experimental import pallas as pl
from jax.experimental.pallas import tpu as pltpu
from jax.sharding import PartitionSpec as P

SIDE = 128
INTERP_TAPS = 8
MAX_SHIFT = 16
BAND_BINS = 16
DOPPLER_BLOCKS = 8
COMPRESS_ROWS = 256
RIM_ROWS = 32
VMEM = 56 * 1024 * 1024


def transform_tables():
    k = np.arange(SIDE)
    angle = 2.0 * np.pi * ((k[:, None] * k[None, :]) % SIDE) / SIDE
    c, s = np.cos(angle), np.sin(angle)
    forward = np.block([[c, s], [-s, c]])
    inverse = np.block([[c, -s], [s, c]])
    twist = 2.0 * np.pi * (k[:, None] * k[None, :]) / (SIDE * SIDE)
    return forward, inverse, np.cos(twist), np.sin(twist)


def split_const(matrix):
    high = jnp.asarray(matrix, jnp.float32).astype(jnp.bfloat16)
    low_np = np.asarray(matrix, np.float64) - np.asarray(
        np.asarray(matrix, np.float32).astype(jnp.bfloat16), np.float64
    )
    return jnp.stack([high, jnp.asarray(low_np, jnp.float32).astype(jnp.bfloat16)])


def split_data(value):
    high = value.astype(jnp.bfloat16)
    return high, (value - high.astype(jnp.float32)).astype(jnp.bfloat16)


NN = (((1,), (0,)), ((), ()))
NT = (((1,), (1,)), ((), ()))
MESH = pl.DeviceIdType.MESH


def mm(a, b, dims):
    return lax.dot_general(a, b, dims, preferred_element_type=jnp.float32)


def mm2(table, data, dims):
    return mm(table[0], data, dims) + mm(table[1], data, dims)


def mm3(table, value, dims):
    high, low = split_data(value)
    return mm(table[0], high, dims) + (mm(table[1], high, dims) + mm(table[0], low, dims))


def phase_starts(bands):
    cuts = [0, max(2, bands * 6 // 16), bands * 11 // 16, bands * 14 // 16]
    return [at for k, at in enumerate(cuts) if k == 0 or at > cuts[k - 1]] + [bands]


def exchange_kernel(
    width, block_rows,
    shift_ref, weight_ref, w_ref, ftable_ref, itable_ref, cos_ref, sin_ref, pcos_ref, psin_ref,
    echoes_ref, turned_ref, inner_ref,
    window, arrived, data, spectrum, moved, staged,
    load_sem, rim_send, rim_recv, out_send, out_recv, halo_send, halo_recv, in_sem, inner_sem, token,
):
    az_count, rg_count = lax.axis_size("az"), lax.axis_size("rg")
    a, g = lax.axis_index("az"), lax.axis_index("rg")
    last, middle = az_count - 1, az_count // 2 - 1
    rows, lines = echoes_ref.shape[1], echoes_ref.shape[2]
    taps = window.shape[1] - rows
    span = w_ref.shape[2]
    local_rows = rows // az_count
    bands = local_rows // BAND_BINS
    starts = phase_starts(bands)
    phases = len(starts) - 1
    chunks = lines // width
    has_before, has_after = g > 0, g < rg_count - 1
    before = lax.rem(g + rg_count - 1, rg_count)
    after = lax.rem(g + 1, rg_count)
    late = lax.rem(g, 2) == 1
    early = jnp.logical_not(late)
    whole_rows, whole_lines = pl.ds(0, local_rows), pl.ds(0, lines)
    halo_rows = pl.ds(local_rows, RIM_ROWS)

    def columns(c):
        return pl.ds(pl.multiple_of(c * width, width), width)

    def own_load(c):
        return pltpu.make_async_copy(
            echoes_ref.at[:, :, columns(c)],
            window.at[:, pl.ds(0, rows), columns(c)],
            load_sem.at[c],
        )

    def rim_copy(c):
        return pltpu.make_async_remote_copy(
            src_ref=echoes_ref.at[:, pl.ds(0, taps), columns(c)],
            dst_ref=window.at[:, pl.ds(rows, taps), columns(c)],
            send_sem=rim_send.at[c],
            recv_sem=rim_recv.at[c],
            device_id=(a, before),
            device_id_type=MESH,
        )

    def start_load(c, _):
        own_load(c).start()
        return 0

    lax.fori_loop(0, chunks, start_load, 0)

    barrier = pltpu.get_barrier_semaphore()

    def greet(az_at, rg_at):
        pl.semaphore_signal(barrier, inc=1, device_id=(az_at, rg_at), device_id_type=MESH)

    def greet_peer(d, _):
        greet(lax.rem(a + d, az_count), g)
        return 0

    lax.fori_loop(1, az_count, greet_peer, 0)

    @pl.when(has_before)
    def _():
        greet(a, before)

    @pl.when(has_after)
    def _():
        greet(a, after)

    @pl.when(has_before & (a != last))
    def _():
        greet(last, before)

    @pl.when(has_after & (a == last))
    def _():
        def greet_halo(b, _):
            greet(b, after)
            return 0

        lax.fori_loop(0, last, greet_halo, 0)

    one = lambda flag: jnp.where(flag, 1, 0)
    pl.semaphore_wait(
        barrier,
        last
        + one(has_before)
        + one(has_after)
        + one(has_before & (a != last))
        + last * one(has_after & (a == last)),
    )

    upfront = jnp.where(late, chunks, min(2, chunks))

    @pl.when(has_before)
    def _():
        def start_rim(c, _):
            rim_copy(c).start()
            return 0

        lax.fori_loop(0, upfront, start_rim, 0)

    @pl.when(jnp.logical_not(has_after))
    def _():
        def clear(i, _):
            at = pl.ds(pl.multiple_of(rows + i * 128, 128), 128)
            window[:, at, :] = jnp.zeros((2, 128, lines), window.dtype)
            return 0

        lax.fori_loop(0, taps // 128, clear, 0)

        @pl.when(a == last)
        def _():
            def clear_halo(b, _):
                pltpu.make_async_copy(
                    window.at[:, pl.ds(rows, RIM_ROWS), :],
                    turned_ref.at[b, :, halo_rows, :],
                    halo_recv.at[0],
                ).start()
                return 0

            lax.fori_loop(0, az_count, clear_halo, 0)

    def rows_of(b, first, height):
        return pl.ds(pl.multiple_of(b * local_rows + first, BAND_BINS), height)

    def block_copy(b, first, height, cols, send, receive):
        return pltpu.make_async_remote_copy(
            src_ref=window.at[:, rows_of(b, first, height), cols],
            dst_ref=turned_ref.at[a, :, pl.ds(first, height), cols],
            send_sem=out_send.at[send],
            recv_sem=out_recv.at[receive],
            device_id=(b, g),
            device_id_type=MESH,
        )

    def send_blocks(first, height, cols, send, receive):
        def one_block(d, _):
            block_copy(lax.rem(a + d, az_count), first, height, cols, send, receive).start()
            return 0

        lax.fori_loop(1, az_count, one_block, 0)
        pltpu.make_async_copy(
            window.at[:, rows_of(a, first, height), cols],
            turned_ref.at[a, :, pl.ds(first, height), cols],
            out_recv.at[receive],
        ).start()

    def sent_blocks(height, cols, send):
        held = window.at[:, pl.ds(0, last * height), cols]
        pltpu.make_async_copy(held, held, out_send.at[send]).wait()

    def halo_copy(first, az_at, rg_at, send):
        return pltpu.make_async_remote_copy(
            src_ref=window.at[:, pl.ds(first, RIM_ROWS), :],
            dst_ref=turned_ref.at[a, :, halo_rows, :],
            send_sem=halo_send.at[send],
            recv_sem=halo_recv.at[0],
            device_id=(az_at, rg_at),
            device_id_type=MESH,
        )

    middle_halo = halo_copy((middle + 1) * local_rows, middle, g, 0)
    outer_halo = halo_copy(0, last, before, 1)
    neighbour_halo = pltpu.make_async_remote_copy(
        src_ref=turned_ref.at[:, :, pl.ds(0, RIM_ROWS), :],
        dst_ref=turned_ref.at[:, :, halo_rows, :],
        send_sem=halo_send.at[2],
        recv_sem=halo_recv.at[0],
        device_id=(lax.rem(a + last, az_count), g),
        device_id_type=MESH,
    )
    passes_halo = (a > 0) & (a != middle + 1)

    def chunk(c, _):
        cols = columns(c)
        own_load(c).wait()

        @pl.when(has_after)
        def _():
            rim_copy(c).wait_recv()

        def block(i, _):
            start = pl.multiple_of(i * block_rows, block_rows)
            total = mm(w_ref[0], window[0, pl.ds(start, span), cols], NN)
            total = total + mm(w_ref[1], window[1, pl.ds(start, span), cols], NN)
            total = total.astype(jnp.bfloat16)
            window[0, pl.ds(start, block_rows), cols] = total[:block_rows]
            window[1, pl.ds(start, block_rows), cols] = total[block_rows:]
            return 0

        lax.fori_loop(0, rows // block_rows, block, 0)

        @pl.when(early)
        def _():
            send_blocks(0, local_rows, cols, c, 0)

        @pl.when(has_before)
        def _():
            rim_copy(c).wait_send()

            @pl.when(c + upfront < chunks)
            def _():
                rim_copy(c + upfront).start()

        return 0

    lax.fori_loop(0, chunks, chunk, 0)

    @pl.when(a == middle)
    def _():
        pltpu.make_async_copy(
            window.at[:, pl.ds((middle + 1) * local_rows, RIM_ROWS), :],
            turned_ref.at[a, :, halo_rows, :],
            halo_recv.at[0],
        ).start()

    @pl.when(a != middle)
    def _():
        middle_halo.start()

    @pl.when(has_before)
    def _():
        outer_halo.start()

    def send_phase(p):
        send_blocks(starts[p] * BAND_BINS, height_of(p), whole_lines, p, p)

    def height_of(p):
        return (starts[p + 1] - starts[p]) * BAND_BINS

    @pl.when(early)
    def _():
        def sent_chunk(c, _):
            sent_blocks(local_rows, columns(c), 0 + c)
            return 0

        lax.fori_loop(0, chunks - 1, sent_chunk, 0)
        pl.semaphore_signal(token, inc=1, device_id=(a, after), device_id_type=MESH)
        sent_chunk(chunks - 1, 0)
        pltpu.make_async_copy(
            turned_ref.at[:, :, whole_rows, :], turned_ref.at[:, :, whole_rows, :], out_recv.at[0]
        ).wait()

    @pl.when(late)
    def _():
        pl.semaphore_wait(token, 1)
        send_phase(0)
        if phases > 1:
            send_phase(1)

    def enter_phase(p):
        @pl.when(late)
        def _():
            sent_blocks(height_of(p), whole_lines, p)
            if p + 2 < phases:
                send_phase(p + 2)
            landed = turned_ref.at[:, :, pl.ds(starts[p] * BAND_BINS, height_of(p)), :]
            pltpu.make_async_copy(landed, landed, out_recv.at[p]).wait()

    total_bands = bands + RIM_ROWS // BAND_BINS
    fresh = RIM_ROWS

    def band_load(i):
        slot = lax.rem(i, 2)
        return pltpu.make_async_copy(
            turned_ref.at[:, :, pl.ds(pl.multiple_of(i * BAND_BINS, BAND_BINS), BAND_BINS), :],
            arrived.at[slot],
            in_sem.at[slot],
        )

    def inner_store(band):
        slot = lax.rem(band, 2)
        return pltpu.make_async_copy(
            staged.at[slot],
            inner_ref.at[pl.ds(pl.multiple_of(band * BAND_BINS, BAND_BINS), BAND_BINS)],
            inner_sem.at[slot],
        )

    def band_step(i, _):
        for p in range(phases):
            @pl.when(i == starts[p])
            def _():
                enter_phase(p)
                if p == 0:
                    @pl.when(passes_halo)
                    def _():
                        neighbour_halo.start()
                band_load(i).start()

        @pl.when(i == bands)
        def _():
            whole_halo = turned_ref.at[:, :, halo_rows, :]
            pltpu.make_async_copy(whole_halo, whole_halo, halo_recv.at[0]).wait()
            band_load(i).start()

        band_load(i).wait()
        opens = i + 1 == total_bands
        for at in starts:
            opens = opens | (i + 1 == at)

        @pl.when(jnp.logical_not(opens))
        def _():
            band_load(i + 1).start()

        forward_band(lax.rem(i, 2), ftable_ref, cos_ref, sin_ref, arrived, data, spectrum, fresh)

        @pl.when(i >= 2)
        def _():
            band = i - 2

            @pl.when(band >= 2)
            def _():
                inner_store(band - 2).wait()

            migrate_band(
                band, shift_ref, weight_ref, itable_ref, cos_ref, sin_ref, pcos_ref, psin_ref,
                spectrum, moved, staged, lax.rem(band, 2),
            )
            inner_store(band).start()

        def slide(r, _):
            spectrum[:, r] = spectrum[:, r + BAND_BINS]
            return 0

        lax.fori_loop(0, fresh, slide, 0)
        return 0

    lax.fori_loop(0, total_bands, band_step, 0)
    for band in range(max(0, bands - 2), bands):
        inner_store(band).wait()

    @pl.when(a != middle)
    def _():
        middle_halo.wait_send()

    @pl.when(has_before)
    def _():
        outer_halo.wait_send()

    @pl.when(passes_halo)
    def _():
        neighbour_halo.wait_send()


def forward_band(slot, table_ref, cos_ref, sin_ref, arrived, data, spectrum, fresh):
    _, az_count, _, rows, lines = arrived.shape
    per = lines // SIDE
    for source in range(az_count):
        for c in range(2):
            piece = arrived[slot, source, c].astype(jnp.float32)
            data[:, c * SIDE + source * per : c * SIDE + (source + 1) * per, :] = piece.reshape(
                rows, per, SIDE
            )

    def pair(i, _):
        both = jnp.concatenate([data[2 * i], data[2 * i + 1]], axis=1).astype(jnp.bfloat16)
        first = mm2(table_ref, both, NN)
        cosine, sine = cos_ref[...], sin_ref[...]
        turned = []
        for k in range(2):
            real = first[:SIDE, k * SIDE : (k + 1) * SIDE]
            imag = first[SIDE:, k * SIDE : (k + 1) * SIDE]
            turned.append(
                jnp.concatenate(
                    [real * cosine + imag * sine, imag * cosine - real * sine], axis=1
                )
            )
        second = mm3(table_ref, jnp.concatenate(turned, axis=0), NT)
        for k in range(2):
            spectrum[0, fresh + 2 * i + k] = second[:SIDE, k * SIDE : (k + 1) * SIDE]
            spectrum[1, fresh + 2 * i + k] = second[SIDE:, k * SIDE : (k + 1) * SIDE]
        return 0

    lax.fori_loop(0, rows // 2, pair, 0, unroll=2)


def migrate_band(
    band, shift_ref, weight_ref, table_ref, cos_ref, sin_ref, pcos_ref, psin_ref,
    window, moved, staged, slot
):
    deep = SIDE // DOPPLER_BLOCKS
    taps = [weight_ref[band, t] for t in range(INTERP_TAPS)]

    def block(d, _):
        shift = shift_ref[band, d]
        spot = pl.ds(pl.multiple_of(d * deep, deep), deep)
        pcos, psin = pcos_ref[band, spot, :], psin_ref[band, spot, :]
        for half in range(2):
            rows = BAND_BINS // 2
            parts = []
            for c in range(2):
                total = taps[0] * window[c, pl.ds(shift + half * rows, rows), spot, :]
                for t in range(1, INTERP_TAPS):
                    total = total + taps[t] * window[c, pl.ds(shift + half * rows + t, rows), spot, :]
                parts.append(total)
            real, imag = parts
            put = slice(half * rows, (half + 1) * rows)
            moved[put, spot, :] = real * pcos + imag * psin
            low = pl.ds(pl.multiple_of(SIDE + d * deep, deep), deep)
            moved[put, low, :] = imag * pcos - real * psin
        return 0

    lax.fori_loop(0, DOPPLER_BLOCKS, block, 0)

    def pair(i, _):
        both = jnp.concatenate([moved[2 * i], moved[2 * i + 1]], axis=1)
        first = mm3(table_ref, both, NN)
        cosine, sine = cos_ref[...], sin_ref[...]
        for k in range(2):
            real = first[:SIDE, k * SIDE : (k + 1) * SIDE]
            imag = first[SIDE:, k * SIDE : (k + 1) * SIDE]
            staged[slot, 2 * i + k, :, :SIDE] = (real * cosine - imag * sine).astype(jnp.bfloat16)
            staged[slot, 2 * i + k, :, SIDE:] = (imag * cosine + real * sine).astype(jnp.bfloat16)
        return 0

    lax.fori_loop(0, BAND_BINS // 2, pair, 0, unroll=2)


def exchange(shifts, live_weight, weights, ftables, itable, pcos, psin, echoes, az_count):
    ftable, cosine, sine = ftables
    rows, lines = echoes.shape[1], echoes.shape[2]
    span = weights.shape[2]
    block_rows = weights.shape[1] // 2
    taps = span - block_rows
    width = math.gcd(256, lines)
    chunks = lines // width
    local_rows = rows // az_count
    phases = len(phase_starts(local_rows // BAND_BINS)) - 1
    vmem = pl.BlockSpec(memory_space=pltpu.VMEM)
    smem = pl.BlockSpec(memory_space=pltpu.SMEM)
    anywhere = pl.BlockSpec(memory_space=pl.ANY)
    dma = pltpu.SemaphoreType.DMA
    return pl.pallas_call(
        functools.partial(exchange_kernel, width, block_rows),
        out_shape=[
            jax.ShapeDtypeStruct((az_count, 2, local_rows + RIM_ROWS, lines), jnp.bfloat16),
            jax.ShapeDtypeStruct((local_rows, SIDE, 2 * SIDE), jnp.bfloat16),
        ],
        in_specs=[smem, smem] + [vmem] * 7 + [anywhere],
        out_specs=[anywhere, anywhere],
        scratch_shapes=[
            pltpu.VMEM((2, rows + taps, lines), jnp.bfloat16),
            pltpu.VMEM((2, az_count, 2, BAND_BINS, lines), jnp.bfloat16),
            pltpu.VMEM((BAND_BINS, 2 * SIDE, SIDE), jnp.float32),
            pltpu.VMEM((2, RIM_ROWS + BAND_BINS, SIDE, SIDE), jnp.float32),
            pltpu.VMEM((BAND_BINS, 2 * SIDE, SIDE), jnp.float32),
            pltpu.VMEM((2, BAND_BINS, SIDE, 2 * SIDE), jnp.bfloat16),
            dma((chunks,)),
            dma((chunks,)),
            dma((chunks,)),
            dma((max(chunks, phases),)),
            dma((phases,)),
            dma((3,)),
            dma((1,)),
            dma((2,)),
            dma((2,)),
            pltpu.SemaphoreType.REGULAR,
        ],
        compiler_params=pltpu.CompilerParams(
            vmem_limit_bytes=60 * 1024 * 1024, collective_id=0, has_side_effects=True
        ),
        cost_estimate=pl.CostEstimate(
            flops=8 * rows * span * lines + local_rows * 8 * 16 * SIDE**3,
            bytes_accessed=4 * lines * (4 * rows + taps),
            transcendentals=0,
        ),
        name="exchange",
    )(shifts, live_weight, weights, ftable, itable, cosine, sine, pcos, psin, echoes)


def finish_kernel(table_ref, inner_ref, out_ref, image):
    def pair(i, _):
        both = jnp.concatenate([inner_ref[2 * i], inner_ref[2 * i + 1]], axis=0)
        second = mm2(table_ref, both, NT) * (1.0 / (SIDE * SIDE))
        for k in range(2):
            image[2 * i + k] = second[:, k * SIDE : (k + 1) * SIDE]
        return 0

    lax.fori_loop(0, BAND_BINS // 2, pair, 0, unroll=2)
    group = 16
    for c in range(2):
        for g in range(SIDE // group):
            piece = image[:, c * SIDE + g * group : c * SIDE + (g + 1) * group, :]
            out_ref[c, :, g * group * SIDE : (g + 1) * group * SIDE] = piece.reshape(
                BAND_BINS, group * SIDE
            )


def finish(table, inner):
    local_rows = inner.shape[0]
    return pl.pallas_call(
        finish_kernel,
        out_shape=jax.ShapeDtypeStruct((2, local_rows, SIDE * SIDE), jnp.float32),
        grid=(local_rows // BAND_BINS,),
        in_specs=[
            pl.BlockSpec(table.shape, lambda i: (0, 0, 0)),
            pl.BlockSpec((BAND_BINS, SIDE, 2 * SIDE), lambda i: (i, 0, 0)),
        ],
        out_specs=pl.BlockSpec((2, BAND_BINS, SIDE * SIDE), lambda i: (0, i, 0)),
        scratch_shapes=[pltpu.VMEM((BAND_BINS, 2 * SIDE, SIDE), jnp.float32)],
        compiler_params=pltpu.CompilerParams(vmem_limit_bytes=VMEM),
        name="finish",
    )(table, inner)


def compress_weights(replica, block_rows):
    taps = replica.shape[1]
    span = taps + block_rows

    def banded(vector):
        cycled = jnp.concatenate([vector, jnp.zeros((span + 1 - taps,), vector.dtype)])
        return jnp.tile(cycled, block_rows)[: block_rows * span].reshape(block_rows, span)

    real_rows = banded(replica[0])
    imag_rows = banded(replica[1])
    return jnp.stack(
        [
            jnp.concatenate([real_rows, -imag_rows], axis=0),
            jnp.concatenate([imag_rows, real_rows], axis=0),
        ]
    )


def per_device(echoes, replica, shifts, tap_counts, interp_weights, fm_rates):
    range_dev = echoes.shape[1]
    az_count = lax.axis_size("az")
    rg_count = lax.axis_size("rg")
    local_rows = range_dev // az_count
    block_rows = COMPRESS_ROWS
    bands_here = local_rows // BAND_BINS
    az_pos = lax.axis_index("az")
    rg_pos = lax.axis_index("rg")

    weights = compress_weights(replica, block_rows)
    forward_m, inverse_m, twist_cos, twist_sin = transform_tables()
    cosine = jnp.asarray(twist_cos, jnp.float32)
    sine = jnp.asarray(twist_sin, jnp.float32)
    forward_tables = (split_const(forward_m), cosine, sine)
    inverse_table = split_const(inverse_m)

    band_first = (rg_pos * range_dev + az_pos * local_rows) // BAND_BINS
    band_shift = lax.dynamic_slice_in_dim(shifts, band_first, bands_here)
    band_taps = lax.dynamic_slice_in_dim(tap_counts, band_first, bands_here)
    band_weight = lax.dynamic_slice_in_dim(interp_weights, band_first, bands_here)
    tap_index = lax.broadcasted_iota(jnp.int32, (bands_here, INTERP_TAPS), 1)
    live_weight = jnp.where(tap_index < band_taps[:, None], band_weight, 0.0)
    band_rate = lax.dynamic_slice_in_dim(fm_rates, band_first, bands_here)
    total_lines = SIDE * SIDE
    doppler = SIDE * lax.broadcasted_iota(jnp.int32, (SIDE, SIDE), 0) + lax.broadcasted_iota(
        jnp.int32, (SIDE, SIDE), 1
    )
    signed = (
        jnp.where(doppler < total_lines // 2, doppler, doppler - total_lines).astype(jnp.float32)
        / total_lines
    )
    phases = math.pi * band_rate[:, None, None] * (signed * signed)[None]
    pcos = jnp.cos(phases)
    psin = jnp.sin(phases)

    _, inner = exchange(
        band_shift, live_weight, weights, forward_tables, inverse_table, pcos, psin, echoes, az_count
    )
    return finish(inverse_table, inner)


def solution(mesh):
    return jax.shard_map(
        per_device,
        mesh=mesh,
        in_specs=(P(None, "rg", "az"), P(), P(), P(), P(), P()),
        out_specs=P(None, ("rg", "az"), None),
        check_vma=False,
    )
```

```python
import functools
import math

import jax
import jax.numpy as jnp
import numpy as np
from jax import lax
from jax.experimental import pallas as pl
from jax.experimental.pallas import tpu as pltpu
from jax.sharding import PartitionSpec as P

SIDE = 128
INTERP_TAPS = 8
MAX_SHIFT = 16
BAND_BINS = 16
DOPPLER_BLOCKS = 8
COMPRESS_ROWS = 256
RIM_ROWS = 32
VMEM = 56 * 1024 * 1024


def transform_tables():
    k = np.arange(SIDE)
    angle = 2.0 * np.pi * ((k[:, None] * k[None, :]) % SIDE) / SIDE
    c, s = np.cos(angle), np.sin(angle)
    forward = np.block([[c, s], [-s, c]])
    inverse = np.block([[c, -s], [s, c]])
    twist = 2.0 * np.pi * (k[:, None] * k[None, :]) / (SIDE * SIDE)
    return forward, inverse, np.cos(twist), np.sin(twist)


def split_const(matrix):
    high = jnp.asarray(matrix, jnp.float32).astype(jnp.bfloat16)
    low_np = np.asarray(matrix, np.float64) - np.asarray(
        np.asarray(matrix, np.float32).astype(jnp.bfloat16), np.float64
    )
    return jnp.stack([high, jnp.asarray(low_np, jnp.float32).astype(jnp.bfloat16)])


def split_data(value):
    high = value.astype(jnp.bfloat16)
    return high, (value - high.astype(jnp.float32)).astype(jnp.bfloat16)


NN = (((1,), (0,)), ((), ()))
NT = (((1,), (1,)), ((), ()))
MESH = pl.DeviceIdType.MESH


def mm(a, b, dims):
    return lax.dot_general(a, b, dims, preferred_element_type=jnp.float32)


def mm2(table, data, dims):
    return mm(table[0], data, dims) + mm(table[1], data, dims)


def mm3(table, value, dims):
    high, low = split_data(value)
    return mm(table[0], high, dims) + (mm(table[1], high, dims) + mm(table[0], low, dims))


def phase_starts(bands):
    return [0] + list(range(2, bands, 3)) + [bands]


def exchange_kernel(
    width, block_rows,
    shift_ref, weight_ref, rate_ref, replica_ref, ftable_ref, itable_ref, cos_ref, sin_ref,
    echoes_ref, turned_ref, inner_ref,
    window, w_ref, arrived, data, spectrum, phase, staged,
    load_sem, rim_send, rim_recv, out_send, out_recv, halo_send, halo_recv, in_sem, inner_sem, token,
):
    az_count, rg_count = lax.axis_size("az"), lax.axis_size("rg")
    a, g = lax.axis_index("az"), lax.axis_index("rg")
    last, middle = az_count - 1, az_count // 2 - 1
    rows, lines = echoes_ref.shape[1], echoes_ref.shape[2]
    taps = window.shape[1] - rows
    span = w_ref.shape[2]
    local_rows = rows // az_count
    bands = local_rows // BAND_BINS
    starts = phase_starts(bands)
    phases = len(starts) - 1
    chunks = lines // width
    has_before, has_after = g > 0, g < rg_count - 1
    before = lax.rem(g + rg_count - 1, rg_count)
    after = lax.rem(g + 1, rg_count)
    late = lax.rem(g, 2) == 1
    early = jnp.logical_not(late)
    whole_rows, whole_lines = pl.ds(0, local_rows), pl.ds(0, lines)
    halo_rows = pl.ds(local_rows, RIM_ROWS)

    def columns(c):
        return pl.ds(pl.multiple_of(c * width, width), width)

    def own_load(c):
        return pltpu.make_async_copy(
            echoes_ref.at[:, :, columns(c)],
            window.at[:, pl.ds(0, rows), columns(c)],
            load_sem.at[c],
        )

    def rim_copy(c):
        return pltpu.make_async_remote_copy(
            src_ref=echoes_ref.at[:, pl.ds(0, taps), columns(c)],
            dst_ref=window.at[:, pl.ds(rows, taps), columns(c)],
            send_sem=rim_send.at[c],
            recv_sem=rim_recv.at[c],
            device_id=(a, before),
            device_id_type=MESH,
        )

    def start_load(c, _):
        own_load(c).start()
        return 0

    lax.fori_loop(0, chunks, start_load, 0)

    barrier = pltpu.get_barrier_semaphore()

    def greet(az_at, rg_at):
        pl.semaphore_signal(barrier, inc=1, device_id=(az_at, rg_at), device_id_type=MESH)

    def greet_peer(d, _):
        greet(lax.rem(a + d, az_count), g)
        return 0

    lax.fori_loop(1, az_count, greet_peer, 0)

    @pl.when(has_before)
    def _():
        greet(a, before)

    @pl.when(has_after)
    def _():
        greet(a, after)

    @pl.when(has_before & (a != last))
    def _():
        greet(last, before)

    @pl.when(has_after & (a == last))
    def _():
        def greet_halo(b, _):
            greet(b, after)
            return 0

        lax.fori_loop(0, last, greet_halo, 0)

    one = lambda flag: jnp.where(flag, 1, 0)
    pl.semaphore_wait(
        barrier,
        last
        + one(has_before)
        + one(has_after)
        + one(has_before & (a != last))
        + last * one(has_after & (a == last)),
    )

    upfront = jnp.where(late, chunks, min(2, chunks))

    @pl.when(has_before)
    def _():
        def start_rim(c, _):
            rim_copy(c).start()
            return 0

        lax.fori_loop(0, upfront, start_rim, 0)

    @pl.when(jnp.logical_not(has_after))
    def _():
        def clear(i, _):
            at = pl.ds(pl.multiple_of(rows + i * 128, 128), 128)
            window[:, at, :] = jnp.zeros((2, 128, lines), window.dtype)
            return 0

        lax.fori_loop(0, taps // 128, clear, 0)

        @pl.when(a == last)
        def _():
            def clear_halo(b, _):
                pltpu.make_async_copy(
                    window.at[:, pl.ds(rows, RIM_ROWS), :],
                    turned_ref.at[b, :, halo_rows, :],
                    halo_recv.at[0],
                ).start()
                return 0

            lax.fori_loop(0, az_count, clear_halo, 0)

    fill_weights(replica_ref, w_ref)

    def rows_of(b, first, height):
        return pl.ds(pl.multiple_of(b * local_rows + first, BAND_BINS), height)

    def block_copy(b, first, height, cols, send, receive):
        return pltpu.make_async_remote_copy(
            src_ref=window.at[:, rows_of(b, first, height), cols],
            dst_ref=turned_ref.at[a, :, pl.ds(first, height), cols],
            send_sem=out_send.at[send],
            recv_sem=out_recv.at[receive],
            device_id=(b, g),
            device_id_type=MESH,
        )

    def send_blocks(first, height, cols, send, receive):
        def one_block(d, _):
            block_copy(lax.rem(a + d, az_count), first, height, cols, send, receive).start()
            return 0

        lax.fori_loop(1, az_count, one_block, 0)
        pltpu.make_async_copy(
            window.at[:, rows_of(a, first, height), cols],
            turned_ref.at[a, :, pl.ds(first, height), cols],
            out_recv.at[receive],
        ).start()

    def sent_blocks(height, cols, send):
        held = window.at[:, pl.ds(0, last * height), cols]
        pltpu.make_async_copy(held, held, out_send.at[send]).wait()

    def halo_copy(first, az_at, rg_at, send):
        return pltpu.make_async_remote_copy(
            src_ref=window.at[:, pl.ds(first, RIM_ROWS), :],
            dst_ref=turned_ref.at[a, :, halo_rows, :],
            send_sem=halo_send.at[send],
            recv_sem=halo_recv.at[0],
            device_id=(az_at, rg_at),
            device_id_type=MESH,
        )

    middle_halo = halo_copy((middle + 1) * local_rows, middle, g, 0)
    outer_halo = halo_copy(0, last, before, 1)
    neighbour_halo = pltpu.make_async_remote_copy(
        src_ref=turned_ref.at[:, :, pl.ds(0, RIM_ROWS), :],
        dst_ref=turned_ref.at[:, :, halo_rows, :],
        send_sem=halo_send.at[2],
        recv_sem=halo_recv.at[0],
        device_id=(lax.rem(a + last, az_count), g),
        device_id_type=MESH,
    )
    passes_halo = (a > 0) & (a != middle + 1)

    def chunk(c, _):
        cols = columns(c)
        own_load(c).wait()

        @pl.when(has_after)
        def _():
            rim_copy(c).wait_recv()

        def block(i, _):
            start = pl.multiple_of(i * block_rows, block_rows)
            total = mm(w_ref[0], window[0, pl.ds(start, span), cols], NN)
            total = total + mm(w_ref[1], window[1, pl.ds(start, span), cols], NN)
            total = total.astype(jnp.bfloat16)
            window[0, pl.ds(start, block_rows), cols] = total[:block_rows]
            window[1, pl.ds(start, block_rows), cols] = total[block_rows:]
            return 0

        lax.fori_loop(0, rows // block_rows, block, 0)

        @pl.when(early)
        def _():
            send_blocks(0, local_rows, cols, c, 0)

        @pl.when(has_before)
        def _():
            rim_copy(c).wait_send()

            @pl.when(c + upfront < chunks)
            def _():
                rim_copy(c + upfront).start()

        return 0

    lax.fori_loop(0, chunks, chunk, 0)

    @pl.when(a == middle)
    def _():
        pltpu.make_async_copy(
            window.at[:, pl.ds((middle + 1) * local_rows, RIM_ROWS), :],
            turned_ref.at[a, :, halo_rows, :],
            halo_recv.at[0],
        ).start()

    @pl.when(a != middle)
    def _():
        middle_halo.start()

    @pl.when(has_before)
    def _():
        outer_halo.start()

    def send_phase(p):
        send_blocks(starts[p] * BAND_BINS, height_of(p), whole_lines, p, p)

    def height_of(p):
        return (starts[p + 1] - starts[p]) * BAND_BINS

    @pl.when(early)
    def _():
        def sent_chunk(c, _):
            sent_blocks(local_rows, columns(c), 0 + c)
            return 0

        lax.fori_loop(0, chunks - 1, sent_chunk, 0)
        pl.semaphore_signal(token, inc=1, device_id=(a, after), device_id_type=MESH)
        sent_chunk(chunks - 1, 0)
        pltpu.make_async_copy(
            turned_ref.at[:, :, whole_rows, :], turned_ref.at[:, :, whole_rows, :], out_recv.at[0]
        ).wait()

    @pl.when(late)
    def _():
        pl.semaphore_wait(token, 1)
        send_phase(0)
        if phases > 1:
            send_phase(1)

    def enter_phase(p):
        @pl.when(late)
        def _():
            sent_blocks(height_of(p), whole_lines, p)
            if p + 2 < phases:
                send_phase(p + 2)
            landed = turned_ref.at[:, :, pl.ds(starts[p] * BAND_BINS, height_of(p)), :]
            pltpu.make_async_copy(landed, landed, out_recv.at[p]).wait()

    total_bands = bands + RIM_ROWS // BAND_BINS
    fresh = RIM_ROWS

    def band_load(i):
        slot = lax.rem(i, 2)
        return pltpu.make_async_copy(
            turned_ref.at[:, :, pl.ds(pl.multiple_of(i * BAND_BINS, BAND_BINS), BAND_BINS), :],
            arrived.at[slot],
            in_sem.at[slot],
        )

    def inner_store(band):
        slot = lax.rem(band, 2)
        return pltpu.make_async_copy(
            staged.at[slot],
            inner_ref.at[pl.ds(pl.multiple_of(band * BAND_BINS, BAND_BINS), BAND_BINS)],
            inner_sem.at[slot],
        )

    def band_step(i, _):
        for p in range(phases):
            @pl.when(i == starts[p])
            def _():
                enter_phase(p)
                if p == 0:
                    @pl.when(passes_halo)
                    def _():
                        neighbour_halo.start()
                band_load(i).start()

        @pl.when(i == bands)
        def _():
            whole_halo = turned_ref.at[:, :, halo_rows, :]
            pltpu.make_async_copy(whole_halo, whole_halo, halo_recv.at[0]).wait()
            band_load(i).start()

        band_load(i).wait()
        opens = i + 1 == total_bands
        for at in starts:
            opens = opens | (i + 1 == at)

        @pl.when(jnp.logical_not(opens))
        def _():
            band_load(i + 1).start()

        forward_band(lax.rem(i, 2), ftable_ref, cos_ref, sin_ref, arrived, data, spectrum, fresh)

        @pl.when(i >= 2)
        def _():
            band = i - 2

            @pl.when(band >= 2)
            def _():
                inner_store(band - 2).wait()

            migrate_band(
                band, shift_ref, weight_ref, rate_ref, itable_ref, cos_ref, sin_ref,
                spectrum, data, phase, staged, lax.rem(band, 2),
            )
            inner_store(band).start()

        def slide(r, _):
            spectrum[:, r] = spectrum[:, r + BAND_BINS]
            return 0

        lax.fori_loop(0, fresh, slide, 0)
        return 0

    lax.fori_loop(0, total_bands, band_step, 0)
    for band in range(max(0, bands - 2), bands):
        inner_store(band).wait()

    @pl.when(a != middle)
    def _():
        middle_halo.wait_send()

    @pl.when(has_before)
    def _():
        outer_halo.wait_send()

    @pl.when(passes_halo)
    def _():
        neighbour_halo.wait_send()


def forward_band(slot, table_ref, cos_ref, sin_ref, arrived, data, spectrum, fresh):
    _, az_count, _, rows, lines = arrived.shape
    per = lines // SIDE
    for source in range(az_count):
        for c in range(2):
            piece = arrived[slot, source, c].astype(jnp.float32)
            data[:, c * SIDE + source * per : c * SIDE + (source + 1) * per, :] = piece.reshape(
                rows, per, SIDE
            )

    both = jnp.concatenate([data[r].astype(jnp.bfloat16) for r in range(rows)], axis=1)
    first = mm2(table_ref, both, NN)
    cosine, sine = cos_ref[...], sin_ref[...]
    turned = []
    for r in range(rows):
        real = first[:SIDE, r * SIDE : (r + 1) * SIDE]
        imag = first[SIDE:, r * SIDE : (r + 1) * SIDE]
        turned.append(
            jnp.concatenate([real * cosine + imag * sine, imag * cosine - real * sine], axis=1)
        )
    second = mm3(table_ref, jnp.concatenate(turned, axis=0), NT)
    for r in range(rows):
        spectrum[0, fresh + r] = second[:SIDE, r * SIDE : (r + 1) * SIDE]
        spectrum[1, fresh + r] = second[SIDE:, r * SIDE : (r + 1) * SIDE]


def migrate_band(
    band, shift_ref, weight_ref, rate_ref, table_ref, cos_ref, sin_ref,
    window, moved, phase, staged, slot
):
    deep = SIDE // DOPPLER_BLOCKS
    total_lines = SIDE * SIDE
    doppler = SIDE * lax.broadcasted_iota(jnp.int32, (SIDE, SIDE), 0) + lax.broadcasted_iota(
        jnp.int32, (SIDE, SIDE), 1
    )
    signed = (
        jnp.where(doppler < total_lines // 2, doppler, doppler - total_lines).astype(jnp.float32)
        / total_lines
    )
    angle = math.pi * rate_ref[band] * (signed * signed)
    phase[0] = jnp.cos(angle)
    phase[1] = jnp.sin(angle)
    taps = [weight_ref[band, t] for t in range(INTERP_TAPS)]

    def block(d, _):
        shift = shift_ref[band, d]
        spot = pl.ds(pl.multiple_of(d * deep, deep), deep)
        pcos, psin = phase[0, spot, :], phase[1, spot, :]
        for half in range(2):
            rows = BAND_BINS // 2
            parts = []
            for c in range(2):
                total = taps[0] * window[c, pl.ds(shift + half * rows, rows), spot, :]
                for t in range(1, INTERP_TAPS):
                    total = total + taps[t] * window[c, pl.ds(shift + half * rows + t, rows), spot, :]
                parts.append(total)
            real, imag = parts
            put = slice(half * rows, (half + 1) * rows)
            moved[put, spot, :] = real * pcos + imag * psin
            low = pl.ds(pl.multiple_of(SIDE + d * deep, deep), deep)
            moved[put, low, :] = imag * pcos - real * psin
        return 0

    lax.fori_loop(0, DOPPLER_BLOCKS, block, 0)

    both = jnp.concatenate([moved[r] for r in range(BAND_BINS)], axis=1)
    first = mm3(table_ref, both, NN)
    cosine, sine = cos_ref[...], sin_ref[...]
    for r in range(BAND_BINS):
        real = first[:SIDE, r * SIDE : (r + 1) * SIDE]
        imag = first[SIDE:, r * SIDE : (r + 1) * SIDE]
        staged[slot, r, :, :SIDE] = (real * cosine - imag * sine).astype(jnp.bfloat16)
        staged[slot, r, :, SIDE:] = (imag * cosine + real * sine).astype(jnp.bfloat16)


def exchange(shifts, live_weight, rates, replica, ftables, itable, echoes, az_count):
    ftable, cosine, sine = ftables
    rows, lines = echoes.shape[1], echoes.shape[2]
    taps = replica.shape[1]
    block_rows = COMPRESS_ROWS
    span = taps + block_rows
    width = math.gcd(256, lines)
    chunks = lines // width
    local_rows = rows // az_count
    phases = len(phase_starts(local_rows // BAND_BINS)) - 1
    vmem = pl.BlockSpec(memory_space=pltpu.VMEM)
    smem = pl.BlockSpec(memory_space=pltpu.SMEM)
    anywhere = pl.BlockSpec(memory_space=pl.ANY)
    dma = pltpu.SemaphoreType.DMA
    return pl.pallas_call(
        functools.partial(exchange_kernel, width, block_rows),
        out_shape=[
            jax.ShapeDtypeStruct((az_count, 2, local_rows + RIM_ROWS, lines), jnp.bfloat16),
            jax.ShapeDtypeStruct((local_rows, SIDE, 2 * SIDE), jnp.bfloat16),
        ],
        in_specs=[smem] * 3 + [vmem] * 5 + [anywhere],
        out_specs=[anywhere, anywhere],
        scratch_shapes=[
            pltpu.VMEM((2, rows + taps, lines), jnp.bfloat16),
            pltpu.VMEM((2, 2 * block_rows, span), jnp.bfloat16),
            pltpu.VMEM((2, az_count, 2, BAND_BINS, lines), jnp.bfloat16),
            pltpu.VMEM((BAND_BINS, 2 * SIDE, SIDE), jnp.float32),
            pltpu.VMEM((2, RIM_ROWS + BAND_BINS, SIDE, SIDE), jnp.float32),
            pltpu.VMEM((2, SIDE, SIDE), jnp.float32),
            pltpu.VMEM((2, BAND_BINS, SIDE, 2 * SIDE), jnp.bfloat16),
            dma((chunks,)),
            dma((chunks,)),
            dma((chunks,)),
            dma((max(chunks, phases),)),
            dma((phases,)),
            dma((3,)),
            dma((1,)),
            dma((2,)),
            dma((2,)),
            pltpu.SemaphoreType.REGULAR,
        ],
        compiler_params=pltpu.CompilerParams(
            vmem_limit_bytes=60 * 1024 * 1024, collective_id=0, has_side_effects=True
        ),
        cost_estimate=pl.CostEstimate(
            flops=8 * rows * span * lines + local_rows * 8 * 16 * SIDE**3,
            bytes_accessed=4 * lines * (4 * rows + taps),
            transcendentals=0,
        ),
        name="exchange",
    )(shifts, live_weight, rates, replica, ftable, itable, cosine, sine, echoes)


def finish_kernel(table_ref, inner_ref, out_ref, image):
    both = jnp.concatenate([inner_ref[r] for r in range(BAND_BINS)], axis=0)
    second = mm2(table_ref, both, NT) * (1.0 / (SIDE * SIDE))
    for r in range(BAND_BINS):
        image[r] = second[:, r * SIDE : (r + 1) * SIDE]
    group = 16
    for c in range(2):
        for g in range(SIDE // group):
            piece = image[:, c * SIDE + g * group : c * SIDE + (g + 1) * group, :]
            out_ref[c, :, g * group * SIDE : (g + 1) * group * SIDE] = piece.reshape(
                BAND_BINS, group * SIDE
            )


def finish(table, inner):
    local_rows = inner.shape[0]
    return pl.pallas_call(
        finish_kernel,
        out_shape=jax.ShapeDtypeStruct((2, local_rows, SIDE * SIDE), jnp.float32),
        grid=(local_rows // BAND_BINS,),
        in_specs=[
            pl.BlockSpec(table.shape, lambda i: (0, 0, 0)),
            pl.BlockSpec((BAND_BINS, SIDE, 2 * SIDE), lambda i: (i, 0, 0)),
        ],
        out_specs=pl.BlockSpec((2, BAND_BINS, SIDE * SIDE), lambda i: (0, i, 0)),
        scratch_shapes=[pltpu.VMEM((BAND_BINS, 2 * SIDE, SIDE), jnp.float32)],
        compiler_params=pltpu.CompilerParams(vmem_limit_bytes=VMEM),
        name="finish",
    )(table, inner)


def fill_weights(replica_ref, w_ref):
    count, span = w_ref.shape[1] // 2, w_ref.shape[2]
    taps = replica_ref[...].astype(jnp.float32)
    for c in range(2):
        padded = jnp.concatenate(
            [taps[c : c + 1], jnp.zeros((1, span - taps.shape[1]), jnp.float32)], axis=1
        )
        rows = pltpu.roll(
            jnp.broadcast_to(padded, (count, span)), 0, 1, stride=1, stride_axis=0
        )
        if c == 0:
            w_ref[0, :count] = rows.astype(jnp.bfloat16)
            w_ref[1, count:] = rows.astype(jnp.bfloat16)
        else:
            w_ref[0, count:] = (-rows).astype(jnp.bfloat16)
            w_ref[1, :count] = rows.astype(jnp.bfloat16)


def per_device(echoes, replica, shifts, tap_counts, interp_weights, fm_rates):
    range_dev = echoes.shape[1]
    az_count = lax.axis_size("az")
    rg_count = lax.axis_size("rg")
    local_rows = range_dev // az_count
    bands_here = local_rows // BAND_BINS
    az_pos = lax.axis_index("az")
    rg_pos = lax.axis_index("rg")

    forward_m, inverse_m, twist_cos, twist_sin = transform_tables()
    cosine = jnp.asarray(twist_cos, jnp.float32)
    sine = jnp.asarray(twist_sin, jnp.float32)
    forward_tables = (split_const(forward_m), cosine, sine)
    inverse_table = split_const(inverse_m)

    band_first = (rg_pos * range_dev + az_pos * local_rows) // BAND_BINS
    band_shift = lax.dynamic_slice_in_dim(shifts, band_first, bands_here)
    band_taps = lax.dynamic_slice_in_dim(tap_counts, band_first, bands_here)
    band_weight = lax.dynamic_slice_in_dim(interp_weights, band_first, bands_here)
    tap_index = lax.broadcasted_iota(jnp.int32, (bands_here, INTERP_TAPS), 1)
    live_weight = jnp.where(tap_index < band_taps[:, None], band_weight, 0.0)
    band_rate = lax.dynamic_slice_in_dim(fm_rates, band_first, bands_here)
    _, inner = exchange(
        band_shift, live_weight, band_rate, replica, forward_tables, inverse_table, echoes, az_count
    )
    return finish(inverse_table, inner)


def solution(mesh):
    return jax.shard_map(
        per_device,
        mesh=mesh,
        in_specs=(P(None, "rg", "az"), P(), P(), P(), P(), P()),
        out_specs=P(None, ("rg", "az"), None),
        check_vma=False,
    )
```

```python
import functools
import math

import jax
import jax.numpy as jnp
import numpy as np
from jax import lax
from jax.experimental import pallas as pl
from jax.experimental.pallas import tpu as pltpu
from jax.sharding import PartitionSpec as P

SIDE = 128
INTERP_TAPS = 8
MAX_SHIFT = 16
BAND_BINS = 16
DOPPLER_BLOCKS = 8
COMPRESS_ROWS = 256
RIM_ROWS = 32
VMEM = 56 * 1024 * 1024


def transform_tables():
    k = np.arange(SIDE)
    angle = 2.0 * np.pi * ((k[:, None] * k[None, :]) % SIDE) / SIDE
    c, s = np.cos(angle), np.sin(angle)
    forward = np.block([[c, s], [-s, c]])
    inverse = np.block([[c, -s], [s, c]])
    twist = 2.0 * np.pi * (k[:, None] * k[None, :]) / (SIDE * SIDE)
    return forward, inverse, np.cos(twist), np.sin(twist)


def split_const(matrix):
    high = jnp.asarray(matrix, jnp.float32).astype(jnp.bfloat16)
    low_np = np.asarray(matrix, np.float64) - np.asarray(
        np.asarray(matrix, np.float32).astype(jnp.bfloat16), np.float64
    )
    return jnp.stack([high, jnp.asarray(low_np, jnp.float32).astype(jnp.bfloat16)])


def split_data(value):
    high = value.astype(jnp.bfloat16)
    return high, (value - high.astype(jnp.float32)).astype(jnp.bfloat16)


NN = (((1,), (0,)), ((), ()))
NT = (((1,), (1,)), ((), ()))
MESH = pl.DeviceIdType.MESH


def mm(a, b, dims):
    return lax.dot_general(a, b, dims, preferred_element_type=jnp.float32)


def mm2(table, data, dims):
    return mm(table[0], data, dims) + mm(table[1], data, dims)


def mm3(table, value, dims):
    high, low = split_data(value)
    return mm(table[0], high, dims) + (mm(table[1], high, dims) + mm(table[0], low, dims))


def phase_starts(bands):
    return [0] + list(range(2, bands - 1, 3)) + [bands - 1, bands]


def exchange_kernel(
    width, block_rows,
    shift_ref, count_ref, weight_ref, rate_ref, replica_ref, ftable_ref, itable_ref, cos_ref, sin_ref,
    echoes_ref, turned_ref, inner_ref,
    window, w_ref, arrived, data, spectrum, phase, staged,
    load_sem, rim_send, rim_recv, out_send, out_recv, halo_send, halo_recv, in_sem, inner_sem, token,
):
    az_count, rg_count = lax.axis_size("az"), lax.axis_size("rg")
    a, g = lax.axis_index("az"), lax.axis_index("rg")
    last, middle = az_count - 1, az_count // 2 - 1
    rows, lines = echoes_ref.shape[1], echoes_ref.shape[2]
    taps = window.shape[1] - rows
    span = w_ref.shape[2]
    local_rows = rows // az_count
    bands = local_rows // BAND_BINS
    starts = phase_starts(bands)
    phases = len(starts) - 1
    chunks = lines // width
    has_before, has_after = g > 0, g < rg_count - 1
    before = lax.rem(g + rg_count - 1, rg_count)
    after = lax.rem(g + 1, rg_count)
    late = lax.rem(g, 2) == 1
    early = jnp.logical_not(late)
    whole_rows, whole_lines = pl.ds(0, local_rows), pl.ds(0, lines)
    halo_rows = pl.ds(local_rows, RIM_ROWS)

    def columns(c):
        return pl.ds(pl.multiple_of(c * width, width), width)

    def own_load(c):
        return pltpu.make_async_copy(
            echoes_ref.at[:, :, columns(c)],
            window.at[:, pl.ds(0, rows), columns(c)],
            load_sem.at[c],
        )

    def rim_copy(c):
        return pltpu.make_async_remote_copy(
            src_ref=echoes_ref.at[:, pl.ds(0, taps), columns(c)],
            dst_ref=window.at[:, pl.ds(rows, taps), columns(c)],
            send_sem=rim_send.at[c],
            recv_sem=rim_recv.at[c],
            device_id=(a, before),
            device_id_type=MESH,
        )

    def start_load(c, _):
        own_load(c).start()
        return 0

    lax.fori_loop(0, chunks, start_load, 0)

    barrier = pltpu.get_barrier_semaphore()

    def greet(az_at, rg_at):
        pl.semaphore_signal(barrier, inc=1, device_id=(az_at, rg_at), device_id_type=MESH)

    def greet_peer(d, _):
        greet(lax.rem(a + d, az_count), g)
        return 0

    lax.fori_loop(1, az_count, greet_peer, 0)

    @pl.when(has_before)
    def _():
        greet(a, before)

    @pl.when(has_after)
    def _():
        greet(a, after)

    @pl.when(has_before & (a != last))
    def _():
        greet(last, before)

    @pl.when(has_after & (a == last))
    def _():
        def greet_halo(b, _):
            greet(b, after)
            return 0

        lax.fori_loop(0, last, greet_halo, 0)

    one = lambda flag: jnp.where(flag, 1, 0)
    pl.semaphore_wait(
        barrier,
        last
        + one(has_before)
        + one(has_after)
        + one(has_before & (a != last))
        + last * one(has_after & (a == last)),
    )

    def rim_sent(c):
        rim_copy(c).wait_send()

        @pl.when(c + 2 < chunks)
        def _():
            rim_copy(c + 2).start()

    @pl.when(has_before)
    def _():
        def start_rim(c, _):
            rim_copy(c).start()
            return 0

        lax.fori_loop(0, min(2, chunks), start_rim, 0)

    fill_weights(replica_ref, w_ref)

    @pl.when(late)
    def _():
        def next_rim(c, _):
            rim_sent(c)
            return 0

        lax.fori_loop(0, chunks, next_rim, 0)

    @pl.when(jnp.logical_not(has_after))
    def _():
        def clear(i, _):
            at = pl.ds(pl.multiple_of(rows + i * 128, 128), 128)
            window[:, at, :] = jnp.zeros((2, 128, lines), window.dtype)
            return 0

        lax.fori_loop(0, taps // 128, clear, 0)

        @pl.when(a == last)
        def _():
            def clear_halo(b, _):
                pltpu.make_async_copy(
                    window.at[:, pl.ds(rows, RIM_ROWS), :],
                    turned_ref.at[b, :, halo_rows, :],
                    halo_recv.at[0],
                ).start()
                return 0

            lax.fori_loop(0, az_count, clear_halo, 0)

    def rows_of(b, first, height):
        return pl.ds(pl.multiple_of(b * local_rows + first, BAND_BINS), height)

    def block_copy(b, first, height, cols, send, receive):
        return pltpu.make_async_remote_copy(
            src_ref=window.at[:, rows_of(b, first, height), cols],
            dst_ref=turned_ref.at[a, :, pl.ds(first, height), cols],
            send_sem=out_send.at[send],
            recv_sem=out_recv.at[receive],
            device_id=(b, g),
            device_id_type=MESH,
        )

    def send_blocks(first, height, cols, send, receive):
        def one_block(d, _):
            block_copy(lax.rem(a + d, az_count), first, height, cols, send, receive).start()
            return 0

        lax.fori_loop(1, az_count, one_block, 0)
        pltpu.make_async_copy(
            window.at[:, rows_of(a, first, height), cols],
            turned_ref.at[a, :, pl.ds(first, height), cols],
            out_recv.at[receive],
        ).start()

    def sent_blocks(height, cols, send):
        held = window.at[:, pl.ds(0, last * height), cols]
        pltpu.make_async_copy(held, held, out_send.at[send]).wait()

    def halo_copy(first, az_at, rg_at, send):
        return pltpu.make_async_remote_copy(
            src_ref=window.at[:, pl.ds(first, RIM_ROWS), :],
            dst_ref=turned_ref.at[a, :, halo_rows, :],
            send_sem=halo_send.at[send],
            recv_sem=halo_recv.at[0],
            device_id=(az_at, rg_at),
            device_id_type=MESH,
        )

    middle_halo = halo_copy((middle + 1) * local_rows, middle, g, 0)
    outer_halo = halo_copy(0, last, before, 1)
    neighbour_halo = pltpu.make_async_remote_copy(
        src_ref=turned_ref.at[:, :, pl.ds(0, RIM_ROWS), :],
        dst_ref=turned_ref.at[:, :, halo_rows, :],
        send_sem=halo_send.at[2],
        recv_sem=halo_recv.at[0],
        device_id=(lax.rem(a + last, az_count), g),
        device_id_type=MESH,
    )
    passes_halo = (a > 0) & (a != middle + 1)

    def chunk(c, _):
        cols = columns(c)
        own_load(c).wait()

        @pl.when(has_after)
        def _():
            rim_copy(c).wait_recv()

        def block(i, _):
            start = pl.multiple_of(i * block_rows, block_rows)
            total = mm(w_ref[0], window[0, pl.ds(start, span), cols], NN)
            total = total + mm(w_ref[1], window[1, pl.ds(start, span), cols], NN)
            total = total.astype(jnp.bfloat16)
            window[0, pl.ds(start, block_rows), cols] = total[:block_rows]
            window[1, pl.ds(start, block_rows), cols] = total[block_rows:]
            return 0

        lax.fori_loop(0, rows // block_rows, block, 0)

        @pl.when(early)
        def _():
            send_blocks(0, local_rows, cols, c, 0)

        @pl.when(has_before & early)
        def _():
            rim_sent(c)

        return 0

    lax.fori_loop(0, chunks, chunk, 0)

    @pl.when(a == middle)
    def _():
        pltpu.make_async_copy(
            window.at[:, pl.ds((middle + 1) * local_rows, RIM_ROWS), :],
            turned_ref.at[a, :, halo_rows, :],
            halo_recv.at[0],
        ).start()

    @pl.when(a != middle)
    def _():
        middle_halo.start()

    @pl.when(has_before)
    def _():
        outer_halo.start()

    def send_phase(p):
        send_blocks(starts[p] * BAND_BINS, height_of(p), whole_lines, p, p)

    def height_of(p):
        return (starts[p + 1] - starts[p]) * BAND_BINS

    @pl.when(early)
    def _():
        def sent_chunk(c, _):
            sent_blocks(local_rows, columns(c), 0 + c)
            return 0

        lax.fori_loop(0, chunks - 1, sent_chunk, 0)
        pl.semaphore_signal(token, inc=1, device_id=(a, after), device_id_type=MESH)
        sent_chunk(chunks - 1, 0)
        pltpu.make_async_copy(
            turned_ref.at[:, :, whole_rows, :], turned_ref.at[:, :, whole_rows, :], out_recv.at[0]
        ).wait()

    @pl.when(late)
    def _():
        pl.semaphore_wait(token, 1)
        send_phase(0)
        if phases > 1:
            send_phase(1)

    def enter_phase(p):
        @pl.when(late)
        def _():
            sent_blocks(height_of(p), whole_lines, p)
            if p + 2 < phases:
                send_phase(p + 2)
            landed = turned_ref.at[:, :, pl.ds(starts[p] * BAND_BINS, height_of(p)), :]
            pltpu.make_async_copy(landed, landed, out_recv.at[p]).wait()

    halo_bands = RIM_ROWS // BAND_BINS
    fresh = RIM_ROWS

    def band_load(i):
        return pltpu.make_async_copy(
            turned_ref.at[:, :, pl.ds(pl.multiple_of(i * BAND_BINS, BAND_BINS), BAND_BINS), :],
            arrived,
            in_sem.at[0],
        )

    def inner_store(band):
        slot = lax.rem(band, 2)
        return pltpu.make_async_copy(
            staged.at[slot],
            inner_ref.at[pl.ds(pl.multiple_of(band * BAND_BINS, BAND_BINS), BAND_BINS)],
            inner_sem.at[slot],
        )

    halo_step = starts[max(phases - 2, 0)]
    band_first = (g * rows + a * local_rows) // BAND_BINS

    def band_step(i, _):
        @pl.when(i == 0)
        def _():
            enter_phase(0)

            @pl.when(passes_halo)
            def _():
                neighbour_halo.start()

        @pl.when(i == halo_step)
        def _():
            whole_halo = turned_ref.at[:, :, halo_rows, :]
            pltpu.make_async_copy(whole_halo, whole_halo, halo_recv.at[0]).wait()

        def transform(k, _):
            is_own = k == halo_bands
            for p in range(1, phases):
                @pl.when(is_own & (i == starts[p]))
                def _():
                    enter_phase(p)

            load = band_load(jnp.where(is_own, i, bands + k))
            load.start()
            load.wait()
            forward_band(
                ftable_ref, cos_ref, sin_ref, arrived, data, spectrum,
                jnp.where(is_own, fresh, fresh + BAND_BINS * (k + 1)),
            )
            return 0

        lax.fori_loop(
            jnp.where(i == halo_step, 0, halo_bands), halo_bands + 1, transform, 0
        )

        def migrate(band, _):
            @pl.when(band >= 2)
            def _():
                inner_store(band - 2).wait()

            migrate_band(
                band_first + band, (band - i + 2) * BAND_BINS, shift_ref, count_ref, weight_ref,
                rate_ref, itable_ref,
                cos_ref, sin_ref, spectrum, data, phase, staged, lax.rem(band, 2),
            )
            inner_store(band).start()
            return 0

        is_last = i == bands - 1
        lax.fori_loop(jnp.maximum(i - 2, 0), jnp.where(is_last, bands, i - 1), migrate, 0)

        def slide(r, _):
            spectrum[:, r] = spectrum[:, r + BAND_BINS]
            return 0

        lax.fori_loop(0, jnp.where(is_last, 0, fresh), slide, 0)
        return 0

    lax.fori_loop(0, bands, band_step, 0)
    for band in range(max(0, bands - 2), bands):
        inner_store(band).wait()

    @pl.when(a != middle)
    def _():
        middle_halo.wait_send()

    @pl.when(has_before)
    def _():
        outer_halo.wait_send()

    @pl.when(passes_halo)
    def _():
        neighbour_halo.wait_send()


def forward_band(table_ref, cos_ref, sin_ref, arrived, data, spectrum, fresh):
    az_count, _, rows, lines = arrived.shape
    per = lines // SIDE
    for source in range(az_count):
        for c in range(2):
            piece = arrived[source, c].astype(jnp.float32)
            data[:, c * SIDE + source * per : c * SIDE + (source + 1) * per, :] = piece.reshape(
                rows, per, SIDE
            )

    both = jnp.concatenate([data[r].astype(jnp.bfloat16) for r in range(rows)], axis=1)
    first = mm2(table_ref, both, NN)
    cosine, sine = cos_ref[...], sin_ref[...]
    turned = []
    for r in range(rows):
        real = first[:SIDE, r * SIDE : (r + 1) * SIDE]
        imag = first[SIDE:, r * SIDE : (r + 1) * SIDE]
        turned.append(
            jnp.concatenate([real * cosine + imag * sine, imag * cosine - real * sine], axis=1)
        )
    second = mm3(table_ref, jnp.concatenate(turned, axis=0), NT)
    for r in range(rows):
        spectrum[0, fresh + r] = second[:SIDE, r * SIDE : (r + 1) * SIDE]
        spectrum[1, fresh + r] = second[SIDE:, r * SIDE : (r + 1) * SIDE]


def migrate_band(
    place, base, shift_ref, count_ref, weight_ref, rate_ref, table_ref, cos_ref, sin_ref,
    window, moved, phase, staged, slot
):
    deep = SIDE // DOPPLER_BLOCKS
    total_lines = SIDE * SIDE
    doppler = SIDE * lax.broadcasted_iota(jnp.int32, (SIDE, SIDE), 0) + lax.broadcasted_iota(
        jnp.int32, (SIDE, SIDE), 1
    )
    signed = (
        jnp.where(doppler < total_lines // 2, doppler, doppler - total_lines).astype(jnp.float32)
        / total_lines
    )
    angle = math.pi * rate_ref[place] * (signed * signed)
    phase[0] = jnp.cos(angle)
    phase[1] = jnp.sin(angle)
    taps = [
        jnp.where(t < count_ref[place], weight_ref[t, place], 0.0) for t in range(INTERP_TAPS)
    ]

    def block(d, _):
        shift = base + shift_ref[d, place]
        spot = pl.ds(pl.multiple_of(d * deep, deep), deep)
        pcos, psin = phase[0, spot, :], phase[1, spot, :]
        for half in range(2):
            rows = BAND_BINS // 2
            parts = []
            for c in range(2):
                total = taps[0] * window[c, pl.ds(shift + half * rows, rows), spot, :]
                for t in range(1, INTERP_TAPS):
                    total = total + taps[t] * window[c, pl.ds(shift + half * rows + t, rows), spot, :]
                parts.append(total)
            real, imag = parts
            put = slice(half * rows, (half + 1) * rows)
            moved[put, spot, :] = real * pcos + imag * psin
            low = pl.ds(pl.multiple_of(SIDE + d * deep, deep), deep)
            moved[put, low, :] = imag * pcos - real * psin
        return 0

    lax.fori_loop(0, DOPPLER_BLOCKS, block, 0)

    both = jnp.concatenate([moved[r] for r in range(BAND_BINS)], axis=1)
    first = mm3(table_ref, both, NN)
    cosine, sine = cos_ref[...], sin_ref[...]
    for r in range(BAND_BINS):
        real = first[:SIDE, r * SIDE : (r + 1) * SIDE]
        imag = first[SIDE:, r * SIDE : (r + 1) * SIDE]
        staged[slot, r, :, :SIDE] = (real * cosine - imag * sine).astype(jnp.bfloat16)
        staged[slot, r, :, SIDE:] = (imag * cosine + real * sine).astype(jnp.bfloat16)


def exchange(shifts, counts, factors, rates, replica, ftables, itable, echoes, az_count):
    ftable, cosine, sine = ftables
    rows, lines = echoes.shape[1], echoes.shape[2]
    taps = replica.shape[1]
    block_rows = COMPRESS_ROWS
    span = taps + block_rows
    width = math.gcd(256, lines)
    chunks = lines // width
    local_rows = rows // az_count
    phases = len(phase_starts(local_rows // BAND_BINS)) - 1
    vmem = pl.BlockSpec(memory_space=pltpu.VMEM)
    smem = pl.BlockSpec(memory_space=pltpu.SMEM)
    anywhere = pl.BlockSpec(memory_space=pl.ANY)
    dma = pltpu.SemaphoreType.DMA
    return pl.pallas_call(
        functools.partial(exchange_kernel, width, block_rows),
        out_shape=[
            jax.ShapeDtypeStruct((az_count, 2, local_rows + RIM_ROWS, lines), jnp.bfloat16),
            jax.ShapeDtypeStruct((local_rows, SIDE, 2 * SIDE), jnp.bfloat16),
        ],
        in_specs=[smem] * 4 + [vmem] * 5 + [anywhere],
        out_specs=[anywhere, anywhere],
        scratch_shapes=[
            pltpu.VMEM((2, rows + taps, lines), jnp.bfloat16),
            pltpu.VMEM((2, 2 * block_rows, span), jnp.bfloat16),
            pltpu.VMEM((az_count, 2, BAND_BINS, lines), jnp.bfloat16),
            pltpu.VMEM((BAND_BINS, 2 * SIDE, SIDE), jnp.float32),
            pltpu.VMEM((2, 2 * RIM_ROWS + BAND_BINS, SIDE, SIDE), jnp.float32),
            pltpu.VMEM((2, SIDE, SIDE), jnp.float32),
            pltpu.VMEM((2, BAND_BINS, SIDE, 2 * SIDE), jnp.bfloat16),
            dma((chunks,)),
            dma((chunks,)),
            dma((chunks,)),
            dma((max(chunks, phases),)),
            dma((phases,)),
            dma((3,)),
            dma((1,)),
            dma((1,)),
            dma((2,)),
            pltpu.SemaphoreType.REGULAR,
        ],
        compiler_params=pltpu.CompilerParams(
            vmem_limit_bytes=60 * 1024 * 1024, collective_id=0, has_side_effects=True
        ),
        cost_estimate=pl.CostEstimate(
            flops=8 * rows * span * lines + local_rows * 8 * 16 * SIDE**3,
            bytes_accessed=4 * lines * (4 * rows + taps),
            transcendentals=0,
        ),
        name="exchange",
    )(shifts.T, counts, factors.T, rates, replica, ftable, itable, cosine, sine, echoes)


def finish_kernel(table_ref, inner_ref, out_ref, image):
    rows = inner_ref.shape[0]
    both = jnp.concatenate([inner_ref[r] for r in range(rows)], axis=0)
    second = mm2(table_ref, both, NT) * (1.0 / (SIDE * SIDE))
    for r in range(rows):
        image[r] = second[:, r * SIDE : (r + 1) * SIDE]
    group = 16
    for c in range(2):
        for g in range(SIDE // group):
            piece = image[:, c * SIDE + g * group : c * SIDE + (g + 1) * group, :]
            out_ref[c, :, g * group * SIDE : (g + 1) * group * SIDE] = piece.reshape(
                rows, group * SIDE
            )


def finish(table, inner):
    local_rows = inner.shape[0]
    rows = math.gcd(32, local_rows)
    return pl.pallas_call(
        finish_kernel,
        out_shape=jax.ShapeDtypeStruct((2, local_rows, SIDE * SIDE), jnp.float32),
        grid=(local_rows // rows,),
        in_specs=[
            pl.BlockSpec(table.shape, lambda i: (0, 0, 0)),
            pl.BlockSpec((rows, SIDE, 2 * SIDE), lambda i: (i, 0, 0)),
        ],
        out_specs=pl.BlockSpec((2, rows, SIDE * SIDE), lambda i: (0, i, 0)),
        scratch_shapes=[pltpu.VMEM((rows, 2 * SIDE, SIDE), jnp.float32)],
        compiler_params=pltpu.CompilerParams(vmem_limit_bytes=VMEM),
        name="finish",
    )(table, inner)


def fill_weights(replica_ref, w_ref):
    count, span = w_ref.shape[1] // 2, w_ref.shape[2]
    taps = replica_ref[...].astype(jnp.float32)
    for c in range(2):
        padded = jnp.concatenate(
            [taps[c : c + 1], jnp.zeros((1, span - taps.shape[1]), jnp.float32)], axis=1
        )
        rows = pltpu.roll(
            jnp.broadcast_to(padded, (count, span)), 0, 1, stride=1, stride_axis=0
        )
        if c == 0:
            w_ref[0, :count] = rows.astype(jnp.bfloat16)
            w_ref[1, count:] = rows.astype(jnp.bfloat16)
        else:
            w_ref[0, count:] = (-rows).astype(jnp.bfloat16)
            w_ref[1, :count] = rows.astype(jnp.bfloat16)


def per_device(echoes, replica, shifts, tap_counts, interp_weights, fm_rates):
    az_count = lax.axis_size("az")
    forward_m, inverse_m, twist_cos, twist_sin = transform_tables()
    cosine = jnp.asarray(twist_cos, jnp.float32)
    sine = jnp.asarray(twist_sin, jnp.float32)
    forward_tables = (split_const(forward_m), cosine, sine)
    inverse_table = split_const(inverse_m)

    _, inner = exchange(
        shifts, tap_counts, interp_weights, fm_rates, replica, forward_tables, inverse_table, echoes, az_count
    )
    return finish(inverse_table, inner)


def solution(mesh):
    return jax.shard_map(
        per_device,
        mesh=mesh,
        in_specs=(P(None, "rg", "az"), P(), P(), P(), P(), P()),
        out_specs=P(None, ("rg", "az"), None),
        check_vma=False,
    )
```

```python
import functools
import math

import jax
import jax.numpy as jnp
import numpy as np
from jax import lax
from jax.experimental import pallas as pl
from jax.experimental.pallas import tpu as pltpu
from jax.sharding import PartitionSpec as P

SIDE = 128
INTERP_TAPS = 8
MAX_SHIFT = 16
BAND_BINS = 16
DOPPLER_BLOCKS = 8
COMPRESS_ROWS = 256
RIM_ROWS = 32
VMEM = 56 * 1024 * 1024


def transform_tables():
    k = np.arange(SIDE)
    angle = 2.0 * np.pi * ((k[:, None] * k[None, :]) % SIDE) / SIDE
    c, s = np.cos(angle), np.sin(angle)
    forward = np.block([[c, s], [-s, c]])
    inverse = np.block([[c, -s], [s, c]])
    twist = 2.0 * np.pi * (k[:, None] * k[None, :]) / (SIDE * SIDE)
    return forward, inverse, np.cos(twist), np.sin(twist)


def split_const(matrix):
    high = jnp.asarray(matrix, jnp.float32).astype(jnp.bfloat16)
    low_np = np.asarray(matrix, np.float64) - np.asarray(
        np.asarray(matrix, np.float32).astype(jnp.bfloat16), np.float64
    )
    return jnp.stack([high, jnp.asarray(low_np, jnp.float32).astype(jnp.bfloat16)])


def split_data(value):
    high = value.astype(jnp.bfloat16)
    return high, (value - high.astype(jnp.float32)).astype(jnp.bfloat16)


NN = (((1,), (0,)), ((), ()))
NT = (((1,), (1,)), ((), ()))
MESH = pl.DeviceIdType.MESH


def mm(a, b, dims):
    return lax.dot_general(a, b, dims, preferred_element_type=jnp.float32)


def mm2(table, data, dims):
    return mm(table[0], data, dims) + mm(table[1], data, dims)


def mm3(table, value, dims):
    high, low = split_data(value)
    return mm(table[0], high, dims) + (mm(table[1], high, dims) + mm(table[0], low, dims))


def phase_starts(bands):
    return list(range(0, bands, 2)) + [bands]


def exchange_kernel(
    width, block_rows,
    shift_ref, count_ref, weight_ref, rate_ref, replica_ref, ftable_ref, itable_ref, cos_ref, sin_ref,
    echoes_ref, turned_ref, inner_ref,
    window, w_ref, arrived, data, spectrum, phase, staged,
    load_sem, rim_send, rim_recv, out_send, out_recv, halo_send, halo_recv, in_sem, inner_sem, token,
):
    az_count, rg_count = lax.axis_size("az"), lax.axis_size("rg")
    a, g = lax.axis_index("az"), lax.axis_index("rg")
    last, middle = az_count - 1, az_count // 2 - 1
    rows, lines = echoes_ref.shape[1], echoes_ref.shape[2]
    taps = window.shape[1] - rows
    span = w_ref.shape[2]
    local_rows = rows // az_count
    bands = local_rows // BAND_BINS
    starts = phase_starts(bands)
    phases = len(starts) - 1
    chunks = lines // width
    has_before, has_after = g > 0, g < rg_count - 1
    before = lax.rem(g + rg_count - 1, rg_count)
    after = lax.rem(g + 1, rg_count)
    late = lax.rem(g, 2) == 1
    early = jnp.logical_not(late)
    whole_rows, whole_lines = pl.ds(0, local_rows), pl.ds(0, lines)
    halo_rows = pl.ds(local_rows, RIM_ROWS)

    def columns(c):
        return pl.ds(pl.multiple_of(c * width, width), width)

    def own_load(c):
        return pltpu.make_async_copy(
            echoes_ref.at[:, :, columns(c)],
            window.at[:, pl.ds(0, rows), columns(c)],
            load_sem.at[c],
        )

    def rim_copy(c):
        return pltpu.make_async_remote_copy(
            src_ref=echoes_ref.at[:, pl.ds(0, taps), columns(c)],
            dst_ref=window.at[:, pl.ds(rows, taps), columns(c)],
            send_sem=rim_send.at[c],
            recv_sem=rim_recv.at[c],
            device_id=(a, before),
            device_id_type=MESH,
        )

    def start_load(c, _):
        own_load(c).start()
        return 0

    lax.fori_loop(0, chunks, start_load, 0)

    barrier = pltpu.get_barrier_semaphore()

    def greet(az_at, rg_at):
        pl.semaphore_signal(barrier, inc=1, device_id=(az_at, rg_at), device_id_type=MESH)

    def greet_peer(d, _):
        greet(lax.rem(a + d, az_count), g)
        return 0

    lax.fori_loop(1, az_count, greet_peer, 0)

    @pl.when(has_before)
    def _():
        greet(a, before)

    @pl.when(has_after)
    def _():
        greet(a, after)

    @pl.when(has_before & (a != last))
    def _():
        greet(last, before)

    @pl.when(has_after & (a == last))
    def _():
        def greet_halo(b, _):
            greet(b, after)
            return 0

        lax.fori_loop(0, last, greet_halo, 0)

    one = lambda flag: jnp.where(flag, 1, 0)
    pl.semaphore_wait(
        barrier,
        last
        + one(has_before)
        + one(has_after)
        + one(has_before & (a != last))
        + last * one(has_after & (a == last)),
    )

    def rim_sent(c):
        rim_copy(c).wait_send()

        @pl.when(c + 2 < chunks)
        def _():
            rim_copy(c + 2).start()

    @pl.when(has_before)
    def _():
        def start_rim(c, _):
            rim_copy(c).start()
            return 0

        lax.fori_loop(0, min(2, chunks), start_rim, 0)

    fill_weights(replica_ref, w_ref)

    @pl.when(late)
    def _():
        def next_rim(c, _):
            rim_sent(c)
            return 0

        lax.fori_loop(0, chunks, next_rim, 0)

    @pl.when(jnp.logical_not(has_after))
    def _():
        def clear(i, _):
            at = pl.ds(pl.multiple_of(rows + i * 128, 128), 128)
            window[:, at, :] = jnp.zeros((2, 128, lines), window.dtype)
            return 0

        lax.fori_loop(0, taps // 128, clear, 0)

        @pl.when(a == last)
        def _():
            def clear_halo(b, _):
                pltpu.make_async_copy(
                    window.at[:, pl.ds(rows, RIM_ROWS), :],
                    turned_ref.at[b, :, halo_rows, :],
                    halo_recv.at[0],
                ).start()
                return 0

            lax.fori_loop(0, az_count, clear_halo, 0)

    def rows_of(b, first, height):
        return pl.ds(pl.multiple_of(b * local_rows + first, BAND_BINS), height)

    def block_copy(b, first, height, cols, send, receive):
        return pltpu.make_async_remote_copy(
            src_ref=window.at[:, rows_of(b, first, height), cols],
            dst_ref=turned_ref.at[a, :, pl.ds(first, height), cols],
            send_sem=out_send.at[send],
            recv_sem=out_recv.at[receive],
            device_id=(b, g),
            device_id_type=MESH,
        )

    def send_blocks(first, height, cols, send, receive):
        def one_block(d, _):
            block_copy(lax.rem(a + d, az_count), first, height, cols, send, receive).start()
            return 0

        lax.fori_loop(1, az_count, one_block, 0)
        pltpu.make_async_copy(
            window.at[:, rows_of(a, first, height), cols],
            turned_ref.at[a, :, pl.ds(first, height), cols],
            out_recv.at[receive],
        ).start()

    def sent_blocks(height, cols, send):
        held = window.at[:, pl.ds(0, last * height), cols]
        pltpu.make_async_copy(held, held, out_send.at[send]).wait()

    def halo_copy(first, az_at, rg_at, send):
        return pltpu.make_async_remote_copy(
            src_ref=window.at[:, pl.ds(first, RIM_ROWS), :],
            dst_ref=turned_ref.at[a, :, halo_rows, :],
            send_sem=halo_send.at[send],
            recv_sem=halo_recv.at[0],
            device_id=(az_at, rg_at),
            device_id_type=MESH,
        )

    middle_halo = halo_copy((middle + 1) * local_rows, middle, g, 0)
    outer_halo = halo_copy(0, last, before, 1)
    neighbour_halo = pltpu.make_async_remote_copy(
        src_ref=turned_ref.at[:, :, pl.ds(0, RIM_ROWS), :],
        dst_ref=turned_ref.at[:, :, halo_rows, :],
        send_sem=halo_send.at[2],
        recv_sem=halo_recv.at[0],
        device_id=(lax.rem(a + last, az_count), g),
        device_id_type=MESH,
    )
    passes_halo = (a > 0) & (a != middle + 1)

    def chunk(c, _):
        cols = columns(c)
        own_load(c).wait()

        @pl.when(has_after)
        def _():
            rim_copy(c).wait_recv()

        def block(i, _):
            start = pl.multiple_of(i * block_rows, block_rows)
            total = mm(w_ref[0], window[0, pl.ds(start, span), cols], NN)
            total = total + mm(w_ref[1], window[1, pl.ds(start, span), cols], NN)
            total = total.astype(jnp.bfloat16)
            window[0, pl.ds(start, block_rows), cols] = total[:block_rows]
            window[1, pl.ds(start, block_rows), cols] = total[block_rows:]
            return 0

        lax.fori_loop(0, rows // block_rows, block, 0)

        @pl.when(early)
        def _():
            send_blocks(0, local_rows, cols, c, 0)

        @pl.when(has_before & early)
        def _():
            rim_sent(c)

        return 0

    lax.fori_loop(0, chunks, chunk, 0)

    @pl.when(a == middle)
    def _():
        pltpu.make_async_copy(
            window.at[:, pl.ds((middle + 1) * local_rows, RIM_ROWS), :],
            turned_ref.at[a, :, halo_rows, :],
            halo_recv.at[0],
        ).start()

    @pl.when(a != middle)
    def _():
        middle_halo.start()

    @pl.when(has_before)
    def _():
        outer_halo.start()

    def send_phase(p):
        send_blocks(starts[p] * BAND_BINS, height_of(p), whole_lines, p, p)

    def height_of(p):
        return (starts[p + 1] - starts[p]) * BAND_BINS

    @pl.when(early)
    def _():
        def sent_chunk(c, _):
            sent_blocks(local_rows, columns(c), 0 + c)
            return 0

        lax.fori_loop(0, chunks - 1, sent_chunk, 0)
        pl.semaphore_signal(token, inc=1, device_id=(a, after), device_id_type=MESH)
        sent_chunk(chunks - 1, 0)
        pltpu.make_async_copy(
            turned_ref.at[:, :, whole_rows, :], turned_ref.at[:, :, whole_rows, :], out_recv.at[0]
        ).wait()

    @pl.when(late)
    def _():
        pl.semaphore_wait(token, 1)
        for p in range(0, min(4, phases)):
            send_phase(p)

    def enter_phase(p):
        @pl.when(late)
        def _():
            sent_blocks(height_of(p), whole_lines, p)
            if p + 4 < phases:
                send_phase(p + 4)
            landed = turned_ref.at[:, :, pl.ds(starts[p] * BAND_BINS, height_of(p)), :]
            pltpu.make_async_copy(landed, landed, out_recv.at[p]).wait()

    halo_bands = RIM_ROWS // BAND_BINS
    fresh = RIM_ROWS

    def band_load(i, slot):
        return pltpu.make_async_copy(
            turned_ref.at[:, :, pl.ds(pl.multiple_of(i * BAND_BINS, BAND_BINS), BAND_BINS), :],
            arrived.at[slot],
            in_sem.at[slot],
        )

    def inner_store(band):
        slot = lax.rem(band, 2)
        return pltpu.make_async_copy(
            staged.at[slot],
            inner_ref.at[pl.ds(pl.multiple_of(band * BAND_BINS, BAND_BINS), BAND_BINS)],
            inner_sem.at[slot],
        )

    halo_step = starts[max(phases - 2, 0)]
    band_first = (g * rows + a * local_rows) // BAND_BINS

    enter_phase(0)

    @pl.when(passes_halo)
    def _():
        neighbour_halo.start()

    band_load(0, 0).start()

    def band_step(i, _):
        @pl.when(i == halo_step)
        def _():
            whole_halo = turned_ref.at[:, :, halo_rows, :]
            pltpu.make_async_copy(whole_halo, whole_halo, halo_recv.at[0]).wait()

        is_last = i == bands - 1
        turn = jnp.where(i < halo_step, lax.rem(i, 3), 0)
        row = fresh + BAND_BINS * turn

        def transform(k, _):
            is_own = k == halo_bands
            slot = lax.rem(jnp.where(is_own, i, i + 1), 2)
            load = band_load(jnp.where(is_own, i, bands + k), slot)

            @pl.when(jnp.logical_not(is_own))
            def _():
                load.start()

            load.wait()
            forward_band(
                slot, ftable_ref, cos_ref, sin_ref, arrived, data, spectrum,
                jnp.where(is_own, row, fresh + BAND_BINS * (k + 1)),
            )
            return 0

        lax.fori_loop(
            jnp.where(i == halo_step, 0, halo_bands), halo_bands + 1, transform, 0
        )

        for p in range(1, phases):
            @pl.when(i + 1 == starts[p])
            def _():
                enter_phase(p)

        @pl.when(jnp.logical_not(is_last))
        def _():
            band_load(i + 1, lax.rem(i + 1, 2)).start()

        def migrate(band, _):
            @pl.when(band >= 2)
            def _():
                inner_store(band - 2).wait()

            migrate_band(
                band_first + band, row - fresh + (band - i + 2) * BAND_BINS, shift_ref, count_ref, weight_ref,
                rate_ref, itable_ref,
                cos_ref, sin_ref, spectrum, data, phase, staged, lax.rem(band, 2),
            )
            inner_store(band).start()
            return 0

        lax.fori_loop(jnp.maximum(i - 2, 0), jnp.where(is_last, bands, i - 1), migrate, 0)

        def slide(r, _):
            spectrum[:, r] = spectrum[:, r + BAND_BINS * (turn + 1)]
            return 0

        full = (turn == 2) | (i >= halo_step - 1)
        lax.fori_loop(0, jnp.where(full & jnp.logical_not(is_last), fresh, 0), slide, 0)
        return 0

    lax.fori_loop(0, bands, band_step, 0)
    for band in range(max(0, bands - 2), bands):
        inner_store(band).wait()

    @pl.when(a != middle)
    def _():
        middle_halo.wait_send()

    @pl.when(has_before)
    def _():
        outer_halo.wait_send()

    @pl.when(passes_halo)
    def _():
        neighbour_halo.wait_send()


def forward_band(slot, table_ref, cos_ref, sin_ref, arrived, data, spectrum, fresh):
    _, az_count, _, rows, lines = arrived.shape
    per = lines // SIDE
    for source in range(az_count):
        for c in range(2):
            piece = arrived[slot, source, c].astype(jnp.float32)
            data[:, c * SIDE + source * per : c * SIDE + (source + 1) * per, :] = piece.reshape(
                rows, per, SIDE
            )

    both = jnp.concatenate([data[r].astype(jnp.bfloat16) for r in range(rows)], axis=1)
    first = mm2(table_ref, both, NN)
    cosine, sine = cos_ref[...], sin_ref[...]
    turned = []
    for r in range(rows):
        real = first[:SIDE, r * SIDE : (r + 1) * SIDE]
        imag = first[SIDE:, r * SIDE : (r + 1) * SIDE]
        turned.append(
            jnp.concatenate([real * cosine + imag * sine, imag * cosine - real * sine], axis=1)
        )
    second = mm3(table_ref, jnp.concatenate(turned, axis=0), NT)
    for r in range(rows):
        spectrum[0, fresh + r] = second[:SIDE, r * SIDE : (r + 1) * SIDE]
        spectrum[1, fresh + r] = second[SIDE:, r * SIDE : (r + 1) * SIDE]


def migrate_band(
    place, base, shift_ref, count_ref, weight_ref, rate_ref, table_ref, cos_ref, sin_ref,
    window, moved, phase, staged, slot
):
    deep = SIDE // DOPPLER_BLOCKS
    total_lines = SIDE * SIDE
    doppler = SIDE * lax.broadcasted_iota(jnp.int32, (SIDE, SIDE), 0) + lax.broadcasted_iota(
        jnp.int32, (SIDE, SIDE), 1
    )
    signed = (
        jnp.where(doppler < total_lines // 2, doppler, doppler - total_lines).astype(jnp.float32)
        / total_lines
    )
    angle = math.pi * rate_ref[place] * (signed * signed)
    phase[0] = jnp.cos(angle)
    phase[1] = jnp.sin(angle)
    taps = [
        jnp.where(t < count_ref[place], weight_ref[t, place], 0.0) for t in range(INTERP_TAPS)
    ]

    def block(d, _):
        shift = base + shift_ref[d, place]
        spot = pl.ds(pl.multiple_of(d * deep, deep), deep)
        pcos, psin = phase[0, spot, :], phase[1, spot, :]
        for half in range(2):
            rows = BAND_BINS // 2
            parts = []
            for c in range(2):
                total = taps[0] * window[c, pl.ds(shift + half * rows, rows), spot, :]
                for t in range(1, INTERP_TAPS):
                    total = total + taps[t] * window[c, pl.ds(shift + half * rows + t, rows), spot, :]
                parts.append(total)
            real, imag = parts
            put = slice(half * rows, (half + 1) * rows)
            moved[put, spot, :] = real * pcos + imag * psin
            low = pl.ds(pl.multiple_of(SIDE + d * deep, deep), deep)
            moved[put, low, :] = imag * pcos - real * psin
        return 0

    lax.fori_loop(0, DOPPLER_BLOCKS, block, 0)

    both = jnp.concatenate([moved[r] for r in range(BAND_BINS)], axis=1)
    first = mm3(table_ref, both, NN)
    cosine, sine = cos_ref[...], sin_ref[...]
    for r in range(BAND_BINS):
        real = first[:SIDE, r * SIDE : (r + 1) * SIDE]
        imag = first[SIDE:, r * SIDE : (r + 1) * SIDE]
        staged[slot, r, :, :SIDE] = (real * cosine - imag * sine).astype(jnp.bfloat16)
        staged[slot, r, :, SIDE:] = (imag * cosine + real * sine).astype(jnp.bfloat16)


def exchange(shifts, counts, factors, rates, replica, ftables, itable, echoes, az_count):
    ftable, cosine, sine = ftables
    rows, lines = echoes.shape[1], echoes.shape[2]
    taps = replica.shape[1]
    block_rows = COMPRESS_ROWS
    span = taps + block_rows
    width = math.gcd(256, lines)
    chunks = lines // width
    local_rows = rows // az_count
    phases = len(phase_starts(local_rows // BAND_BINS)) - 1
    vmem = pl.BlockSpec(memory_space=pltpu.VMEM)
    smem = pl.BlockSpec(memory_space=pltpu.SMEM)
    anywhere = pl.BlockSpec(memory_space=pl.ANY)
    dma = pltpu.SemaphoreType.DMA
    return pl.pallas_call(
        functools.partial(exchange_kernel, width, block_rows),
        out_shape=[
            jax.ShapeDtypeStruct((az_count, 2, local_rows + RIM_ROWS, lines), jnp.bfloat16),
            jax.ShapeDtypeStruct((local_rows, SIDE, 2 * SIDE), jnp.bfloat16),
        ],
        in_specs=[smem] * 4 + [vmem] * 5 + [anywhere],
        out_specs=[anywhere, anywhere],
        scratch_shapes=[
            pltpu.VMEM((2, rows + taps, lines), jnp.bfloat16),
            pltpu.VMEM((2, 2 * block_rows, span), jnp.bfloat16),
            pltpu.VMEM((2, az_count, 2, BAND_BINS, lines), jnp.bfloat16),
            pltpu.VMEM((BAND_BINS, 2 * SIDE, SIDE), jnp.float32),
            pltpu.VMEM((2, 2 * RIM_ROWS + BAND_BINS, SIDE, SIDE), jnp.float32),
            pltpu.VMEM((2, SIDE, SIDE), jnp.float32),
            pltpu.VMEM((2, BAND_BINS, SIDE, 2 * SIDE), jnp.bfloat16),
            dma((chunks,)),
            dma((chunks,)),
            dma((chunks,)),
            dma((max(chunks, phases),)),
            dma((phases,)),
            dma((3,)),
            dma((1,)),
            dma((2,)),
            dma((2,)),
            pltpu.SemaphoreType.REGULAR,
        ],
        compiler_params=pltpu.CompilerParams(
            vmem_limit_bytes=60 * 1024 * 1024, collective_id=0, has_side_effects=True
        ),
        cost_estimate=pl.CostEstimate(
            flops=8 * rows * span * lines + local_rows * 8 * 16 * SIDE**3,
            bytes_accessed=4 * lines * (4 * rows + taps),
            transcendentals=0,
        ),
        name="exchange",
    )(shifts.T, counts, factors.T, rates, replica, ftable, itable, cosine, sine, echoes)


def finish_kernel(table_ref, inner_ref, out_ref, image):
    rows = inner_ref.shape[0]
    both = jnp.concatenate([inner_ref[r] for r in range(rows)], axis=0)
    second = mm2(table_ref, both, NT) * (1.0 / (SIDE * SIDE))
    for r in range(rows):
        image[r] = second[:, r * SIDE : (r + 1) * SIDE]
    group = 16
    for c in range(2):
        for g in range(SIDE // group):
            piece = image[:, c * SIDE + g * group : c * SIDE + (g + 1) * group, :]
            out_ref[c, :, g * group * SIDE : (g + 1) * group * SIDE] = piece.reshape(
                rows, group * SIDE
            )


def finish(table, inner):
    local_rows = inner.shape[0]
    rows = math.gcd(32, local_rows)
    return pl.pallas_call(
        finish_kernel,
        out_shape=jax.ShapeDtypeStruct((2, local_rows, SIDE * SIDE), jnp.float32),
        grid=(local_rows // rows,),
        in_specs=[
            pl.BlockSpec(table.shape, lambda i: (0, 0, 0)),
            pl.BlockSpec((rows, SIDE, 2 * SIDE), lambda i: (i, 0, 0)),
        ],
        out_specs=pl.BlockSpec((2, rows, SIDE * SIDE), lambda i: (0, i, 0)),
        scratch_shapes=[pltpu.VMEM((rows, 2 * SIDE, SIDE), jnp.float32)],
        compiler_params=pltpu.CompilerParams(vmem_limit_bytes=VMEM),
        name="finish",
    )(table, inner)


def fill_weights(replica_ref, w_ref):
    count, span = w_ref.shape[1] // 2, w_ref.shape[2]
    taps = replica_ref[...].astype(jnp.float32)
    for c in range(2):
        padded = jnp.concatenate(
            [taps[c : c + 1], jnp.zeros((1, span - taps.shape[1]), jnp.float32)], axis=1
        )
        rows = pltpu.roll(
            jnp.broadcast_to(padded, (count, span)), 0, 1, stride=1, stride_axis=0
        )
        if c == 0:
            w_ref[0, :count] = rows.astype(jnp.bfloat16)
            w_ref[1, count:] = rows.astype(jnp.bfloat16)
        else:
            w_ref[0, count:] = (-rows).astype(jnp.bfloat16)
            w_ref[1, :count] = rows.astype(jnp.bfloat16)


def per_device(echoes, replica, shifts, tap_counts, interp_weights, fm_rates):
    az_count = lax.axis_size("az")
    forward_m, inverse_m, twist_cos, twist_sin = transform_tables()
    cosine = jnp.asarray(twist_cos, jnp.float32)
    sine = jnp.asarray(twist_sin, jnp.float32)
    forward_tables = (split_const(forward_m), cosine, sine)
    inverse_table = split_const(inverse_m)

    _, inner = exchange(
        shifts, tap_counts, interp_weights, fm_rates, replica, forward_tables, inverse_table, echoes, az_count
    )
    return finish(inverse_table, inner)


def solution(mesh):
    return jax.shard_map(
        per_device,
        mesh=mesh,
        in_specs=(P(None, "rg", "az"), P(), P(), P(), P(), P()),
        out_specs=P(None, ("rg", "az"), None),
        check_vma=False,
    )
```

```python
import functools
import math

import jax
import jax.numpy as jnp
import numpy as np
from jax import lax
from jax.experimental import pallas as pl
from jax.experimental.pallas import tpu as pltpu
from jax.sharding import PartitionSpec as P

SIDE = 128
INTERP_TAPS = 8
MAX_SHIFT = 16
BAND_BINS = 16
DOPPLER_BLOCKS = 8
COMPRESS_ROWS = 256
RIM_ROWS = 32
VMEM = 56 * 1024 * 1024


def transform_tables():
    k = np.arange(SIDE)
    angle = 2.0 * np.pi * ((k[:, None] * k[None, :]) % SIDE) / SIDE
    c, s = np.cos(angle), np.sin(angle)
    forward = np.block([[c, s], [-s, c]])
    inverse = np.block([[c, -s], [s, c]])
    twist = 2.0 * np.pi * (k[:, None] * k[None, :]) / (SIDE * SIDE)
    return forward, inverse, np.cos(twist), np.sin(twist)


def split_const(matrix):
    high = jnp.asarray(matrix, jnp.float32).astype(jnp.bfloat16)
    low_np = np.asarray(matrix, np.float64) - np.asarray(
        np.asarray(matrix, np.float32).astype(jnp.bfloat16), np.float64
    )
    return jnp.stack([high, jnp.asarray(low_np, jnp.float32).astype(jnp.bfloat16)])


def split_data(value):
    high = value.astype(jnp.bfloat16)
    return high, (value - high.astype(jnp.float32)).astype(jnp.bfloat16)


NN = (((1,), (0,)), ((), ()))
NT = (((1,), (1,)), ((), ()))
MESH = pl.DeviceIdType.MESH


def mm(a, b, dims):
    return lax.dot_general(a, b, dims, preferred_element_type=jnp.float32)


def mm2(table, data, dims):
    return mm(table[0], data, dims) + mm(table[1], data, dims)


def mm3(table, value, dims):
    high, low = split_data(value)
    return mm(table[0], high, dims) + (mm(table[1], high, dims) + mm(table[0], low, dims))


def phase_starts(bands):
    return list(range(0, bands - 1, 2)) + [bands - 1, bands]


def exchange_kernel(
    width, block_rows,
    shift_ref, count_ref, weight_ref, rate_ref, replica_ref, ftable_ref, itable_ref, cos_ref, sin_ref,
    echoes_ref, turned_ref, inner_ref,
    window, ahead, w_ref, arrived, data, spectrum, phase, staged,
    load_sem, rim_send, rim_recv, out_send, out_recv, halo_send, halo_recv, in_sem, inner_sem, token,
):
    az_count, rg_count = lax.axis_size("az"), lax.axis_size("rg")
    a, g = lax.axis_index("az"), lax.axis_index("rg")
    last, middle = az_count - 1, az_count // 2 - 1
    rows, lines = echoes_ref.shape[1], echoes_ref.shape[2]
    taps = window.shape[1] - rows
    span = w_ref.shape[2]
    local_rows = rows // az_count
    bands = local_rows // BAND_BINS
    starts = phase_starts(bands)
    phases = len(starts) - 1
    chunks = lines // width
    has_before, has_after = g > 0, g < rg_count - 1
    before = lax.rem(g + rg_count - 1, rg_count)
    after = lax.rem(g + 1, rg_count)
    late = lax.rem(g, 2) == 1
    early = jnp.logical_not(late)
    whole_rows, whole_lines = pl.ds(0, local_rows), pl.ds(0, lines)
    halo_rows = pl.ds(local_rows, RIM_ROWS)

    def columns(c):
        return pl.ds(pl.multiple_of(c * width, width), width)

    def own_load(c):
        return pltpu.make_async_copy(
            echoes_ref.at[:, :, columns(c)],
            window.at[:, pl.ds(0, rows), columns(c)],
            load_sem.at[c],
        )

    def rim_copy(c):
        return pltpu.make_async_remote_copy(
            src_ref=echoes_ref.at[:, pl.ds(0, taps), columns(c)],
            dst_ref=window.at[:, pl.ds(rows, taps), columns(c)],
            send_sem=rim_send.at[c],
            recv_sem=rim_recv.at[c],
            device_id=(a, before),
            device_id_type=MESH,
        )

    def start_load(c, _):
        own_load(c).start()
        return 0

    lax.fori_loop(0, chunks, start_load, 0)

    barrier = pltpu.get_barrier_semaphore()

    def greet(az_at, rg_at):
        pl.semaphore_signal(barrier, inc=1, device_id=(az_at, rg_at), device_id_type=MESH)

    def greet_peer(d, _):
        greet(lax.rem(a + d, az_count), g)
        return 0

    lax.fori_loop(1, az_count, greet_peer, 0)

    @pl.when(has_before)
    def _():
        greet(a, before)

    @pl.when(has_after)
    def _():
        greet(a, after)

    @pl.when(has_before & (a != last))
    def _():
        greet(last, before)

    @pl.when(has_after & (a == last))
    def _():
        def greet_halo(b, _):
            greet(b, after)
            return 0

        lax.fori_loop(0, last, greet_halo, 0)

    one = lambda flag: jnp.where(flag, 1, 0)
    pl.semaphore_wait(
        barrier,
        last
        + one(has_before)
        + one(has_after)
        + one(has_before & (a != last))
        + last * one(has_after & (a == last)),
    )

    flying = jnp.where(late, min(2, chunks), min(4, chunks))

    def rim_sent(c):
        rim_copy(c).wait_send()

        @pl.when(c + flying < chunks)
        def _():
            rim_copy(c + flying).start()

    @pl.when(has_before)
    def _():
        def start_rim(c, _):
            rim_copy(c).start()
            return 0

        lax.fori_loop(0, flying, start_rim, 0)

    fill_weights(replica_ref, w_ref)

    @pl.when(late)
    def _():
        def next_rim(c, _):
            rim_sent(c)
            return 0

        lax.fori_loop(0, chunks, next_rim, 0)

    @pl.when(jnp.logical_not(has_after))
    def _():
        def clear(i, _):
            at = pl.ds(pl.multiple_of(rows + i * 128, 128), 128)
            window[:, at, :] = jnp.zeros((2, 128, lines), window.dtype)
            return 0

        lax.fori_loop(0, taps // 128, clear, 0)

        @pl.when(a == last)
        def _():
            def clear_halo(b, _):
                pltpu.make_async_copy(
                    window.at[:, pl.ds(rows, RIM_ROWS), :],
                    turned_ref.at[b, :, halo_rows, :],
                    halo_recv.at[0],
                ).start()
                return 0

            lax.fori_loop(0, az_count, clear_halo, 0)

    def rows_of(b, first, height):
        return pl.ds(pl.multiple_of(b * local_rows + first, BAND_BINS), height)

    def block_copy(b, first, height, cols, send, receive):
        return pltpu.make_async_remote_copy(
            src_ref=window.at[:, rows_of(b, first, height), cols],
            dst_ref=turned_ref.at[a, :, pl.ds(first, height), cols],
            send_sem=out_send.at[send],
            recv_sem=out_recv.at[receive],
            device_id=(b, g),
            device_id_type=MESH,
        )

    def send_blocks(first, height, cols, send, receive):
        def one_block(d, _):
            block_copy(lax.rem(a + d, az_count), first, height, cols, send, receive).start()
            return 0

        lax.fori_loop(1, az_count, one_block, 0)
        pltpu.make_async_copy(
            window.at[:, rows_of(a, first, height), cols],
            turned_ref.at[a, :, pl.ds(first, height), cols],
            out_recv.at[receive],
        ).start()

    def sent_blocks(height, cols, send):
        held = window.at[:, pl.ds(0, last * height), cols]
        pltpu.make_async_copy(held, held, out_send.at[send]).wait()

    def halo_copy(first, az_at, rg_at, send):
        return pltpu.make_async_remote_copy(
            src_ref=window.at[:, pl.ds(first, RIM_ROWS), :],
            dst_ref=turned_ref.at[a, :, halo_rows, :],
            send_sem=halo_send.at[send],
            recv_sem=halo_recv.at[0],
            device_id=(az_at, rg_at),
            device_id_type=MESH,
        )

    middle_halo = halo_copy((middle + 1) * local_rows, middle, g, 0)
    outer_halo = halo_copy(0, last, before, 1)
    neighbour_halo = pltpu.make_async_remote_copy(
        src_ref=turned_ref.at[:, :, pl.ds(0, RIM_ROWS), :],
        dst_ref=turned_ref.at[:, :, halo_rows, :],
        send_sem=halo_send.at[2],
        recv_sem=halo_recv.at[0],
        device_id=(lax.rem(a + last, az_count), g),
        device_id_type=MESH,
    )
    passes_halo = (a > 0) & (a != middle + 1)

    half_rows = rows // 2
    half_blocks = half_rows // block_rows

    def send_half(source, skipped, first_dest, cols, c):
        here = cols if source is window else pl.ds(0, width)

        def one_block(d, _):
            b = first_dest + lax.rem(a + d, az_count // 2)
            source_rows = pl.ds(
                pl.multiple_of(b * local_rows - skipped, BAND_BINS), local_rows
            )
            target = turned_ref.at[a, :, whole_rows, cols]

            @pl.when(b == a)
            def _():
                pltpu.make_async_copy(
                    source.at[:, source_rows, here], target, out_recv.at[0]
                ).start()

            @pl.when(b != a)
            def _():
                pltpu.make_async_remote_copy(
                    src_ref=source.at[:, source_rows, here],
                    dst_ref=target,
                    send_sem=out_send.at[c],
                    recv_sem=out_recv.at[0],
                    device_id=(b, g),
                    device_id_type=MESH,
                ).start()

            return 0

        lax.fori_loop(0, az_count // 2, one_block, 0)

    def chunk(c, _):
        cols = columns(c)
        own_load(c).wait()

        @pl.when(has_after)
        def _():
            rim_copy(c).wait_recv()

        swapped = (c == 0) & (a <= middle)

        def block(k, _):
            i = lax.rem(k + jnp.where(swapped, half_blocks, 0), 2 * half_blocks)
            start = pl.multiple_of(i * block_rows, block_rows)
            total = mm(w_ref[0], window[0, pl.ds(start, span), cols], NN)
            total = total + mm(w_ref[1], window[1, pl.ds(start, span), cols], NN)
            total = total.astype(jnp.bfloat16)

            @pl.when(swapped & (i >= half_blocks))
            def _():
                held = pl.ds(pl.multiple_of(start - half_rows, block_rows), block_rows)
                ahead[0, held, :] = total[:block_rows]
                ahead[1, held, :] = total[block_rows:]

            @pl.when(jnp.logical_not(swapped & (i >= half_blocks)))
            def _():
                window[0, pl.ds(start, block_rows), cols] = total[:block_rows]
                window[1, pl.ds(start, block_rows), cols] = total[block_rows:]

            return 0

        lax.fori_loop(0, half_blocks, block, 0)

        @pl.when(early & jnp.logical_not(swapped))
        def _():
            send_half(window, 0, 0, cols, c)

        @pl.when(early & swapped)
        def _():
            send_half(ahead, half_rows, az_count // 2, cols, c)

        lax.fori_loop(half_blocks, 2 * half_blocks, block, 0)

        @pl.when(swapped)
        def _():
            window[:, half_rows:rows, cols] = ahead[...]

        @pl.when(early & jnp.logical_not(swapped))
        def _():
            send_half(window, 0, az_count // 2, cols, c)

        @pl.when(early & swapped)
        def _():
            send_half(window, 0, 0, cols, c)

        @pl.when(has_before & early & (c >= 2))
        def _():
            rim_sent(c - 2)

        return 0

    lax.fori_loop(0, chunks, chunk, 0)

    @pl.when(a == middle)
    def _():
        pltpu.make_async_copy(
            window.at[:, pl.ds((middle + 1) * local_rows, RIM_ROWS), :],
            turned_ref.at[a, :, halo_rows, :],
            halo_recv.at[0],
        ).start()

    @pl.when(a != middle)
    def _():
        middle_halo.start()

    @pl.when(has_before)
    def _():
        outer_halo.start()

    def send_phase(p):
        send_blocks(starts[p] * BAND_BINS, height_of(p), whole_lines, p, p)

    @pl.when(has_before & early)
    def _():
        for c in range(max(0, chunks - 2), chunks):
            rim_copy(c).wait_send()

    def height_of(p):
        return (starts[p + 1] - starts[p]) * BAND_BINS

    @pl.when(early)
    def _():
        def sent_chunk(c, _):
            sent_blocks(local_rows, columns(c), 0 + c)
            return 0

        lax.fori_loop(0, chunks - 1, sent_chunk, 0)
        pl.semaphore_signal(token, inc=1, device_id=(a, after), device_id_type=MESH)
        sent_chunk(chunks - 1, 0)
        pltpu.make_async_copy(
            turned_ref.at[:, :, whole_rows, :], turned_ref.at[:, :, whole_rows, :], out_recv.at[0]
        ).wait()

    @pl.when(late)
    def _():
        pl.semaphore_wait(token, 1)
        for p in range(0, min(4, phases)):
            send_phase(p)

    def enter_phase(p):
        @pl.when(late)
        def _():
            sent_blocks(height_of(p), whole_lines, p)
            if p + 4 < phases:
                send_phase(p + 4)
            landed = turned_ref.at[:, :, pl.ds(starts[p] * BAND_BINS, height_of(p)), :]
            pltpu.make_async_copy(landed, landed, out_recv.at[p]).wait()

    halo_bands = RIM_ROWS // BAND_BINS
    fresh = RIM_ROWS

    def band_load(i, slot):
        return pltpu.make_async_copy(
            turned_ref.at[:, :, pl.ds(pl.multiple_of(i * BAND_BINS, BAND_BINS), BAND_BINS), :],
            arrived.at[slot],
            in_sem.at[slot],
        )

    def inner_store(band):
        slot = lax.rem(band, 2)
        return pltpu.make_async_copy(
            staged.at[slot],
            inner_ref.at[pl.ds(pl.multiple_of(band * BAND_BINS, BAND_BINS), BAND_BINS)],
            inner_sem.at[slot],
        )

    halo_step = starts[max(phases - 2, 0)]
    band_first = (g * rows + a * local_rows) // BAND_BINS

    enter_phase(0)

    @pl.when(passes_halo)
    def _():
        neighbour_halo.start()

    band_load(0, 0).start()

    def band_step(i, _):
        @pl.when(i == halo_step)
        def _():
            whole_halo = turned_ref.at[:, :, halo_rows, :]
            pltpu.make_async_copy(whole_halo, whole_halo, halo_recv.at[0]).wait()

        is_last = i == bands - 1
        turn = jnp.where(i < halo_step, lax.rem(i, 3), 0)
        row = fresh + BAND_BINS * turn

        def transform(k, _):
            is_own = k == halo_bands
            slot = lax.rem(jnp.where(is_own, i, i + 1), 2)
            load = band_load(jnp.where(is_own, i, bands + k), slot)

            @pl.when(jnp.logical_not(is_own))
            def _():
                load.start()

            load.wait()
            forward_band(
                slot, ftable_ref, cos_ref, sin_ref, arrived, data, spectrum,
                jnp.where(is_own, row, fresh + BAND_BINS * (k + 1)),
            )
            return 0

        lax.fori_loop(
            jnp.where(i == halo_step, 0, halo_bands), halo_bands + 1, transform, 0
        )

        for p in range(1, phases):
            @pl.when(i + 1 == starts[p])
            def _():
                enter_phase(p)

        @pl.when(jnp.logical_not(is_last))
        def _():
            band_load(i + 1, lax.rem(i + 1, 2)).start()

        def migrate(band, _):
            @pl.when(band >= 2)
            def _():
                inner_store(band - 2).wait()

            migrate_band(
                band_first + band, row - fresh + (band - i + 2) * BAND_BINS, shift_ref, count_ref, weight_ref,
                rate_ref, itable_ref,
                cos_ref, sin_ref, spectrum, data, phase, staged, lax.rem(band, 2),
            )
            inner_store(band).start()
            return 0

        lax.fori_loop(jnp.maximum(i - 2, 0), jnp.where(is_last, bands, i - 1), migrate, 0)

        def slide(r, _):
            spectrum[:, r] = spectrum[:, r + BAND_BINS * (turn + 1)]
            return 0

        full = (turn == 2) | (i >= halo_step - 1)
        lax.fori_loop(0, jnp.where(full & jnp.logical_not(is_last), fresh, 0), slide, 0)
        return 0

    lax.fori_loop(0, bands, band_step, 0)
    for band in range(max(0, bands - 2), bands):
        inner_store(band).wait()

    @pl.when(a != middle)
    def _():
        middle_halo.wait_send()

    @pl.when(has_before)
    def _():
        outer_halo.wait_send()

    @pl.when(passes_halo)
    def _():
        neighbour_halo.wait_send()


def forward_band(slot, table_ref, cos_ref, sin_ref, arrived, data, spectrum, fresh):
    _, az_count, _, rows, lines = arrived.shape
    per = lines // SIDE
    for source in range(az_count):
        for c in range(2):
            piece = arrived[slot, source, c].astype(jnp.float32)
            data[:, c * SIDE + source * per : c * SIDE + (source + 1) * per, :] = piece.reshape(
                rows, per, SIDE
            )

    both = jnp.concatenate([data[r].astype(jnp.bfloat16) for r in range(rows)], axis=1)
    first = mm2(table_ref, both, NN)
    cosine, sine = cos_ref[...], sin_ref[...]
    turned = []
    for r in range(rows):
        real = first[:SIDE, r * SIDE : (r + 1) * SIDE]
        imag = first[SIDE:, r * SIDE : (r + 1) * SIDE]
        turned.append(
            jnp.concatenate([real * cosine + imag * sine, imag * cosine - real * sine], axis=1)
        )
    second = mm3(table_ref, jnp.concatenate(turned, axis=0), NT)
    for r in range(rows):
        spectrum[0, fresh + r] = second[:SIDE, r * SIDE : (r + 1) * SIDE]
        spectrum[1, fresh + r] = second[SIDE:, r * SIDE : (r + 1) * SIDE]


def migrate_band(
    place, base, shift_ref, count_ref, weight_ref, rate_ref, table_ref, cos_ref, sin_ref,
    window, moved, phase, staged, slot
):
    deep = SIDE // DOPPLER_BLOCKS
    total_lines = SIDE * SIDE
    doppler = SIDE * lax.broadcasted_iota(jnp.int32, (SIDE, SIDE), 0) + lax.broadcasted_iota(
        jnp.int32, (SIDE, SIDE), 1
    )
    signed = (
        jnp.where(doppler < total_lines // 2, doppler, doppler - total_lines).astype(jnp.float32)
        / total_lines
    )
    angle = math.pi * rate_ref[place] * (signed * signed)
    phase[0] = jnp.cos(angle)
    phase[1] = jnp.sin(angle)
    taps = [
        jnp.where(t < count_ref[place], weight_ref[t, place], 0.0) for t in range(INTERP_TAPS)
    ]

    def block(d, _):
        shift = base + shift_ref[d, place]
        spot = pl.ds(pl.multiple_of(d * deep, deep), deep)
        pcos, psin = phase[0, spot, :], phase[1, spot, :]
        for half in range(2):
            rows = BAND_BINS // 2
            parts = []
            for c in range(2):
                total = taps[0] * window[c, pl.ds(shift + half * rows, rows), spot, :]
                for t in range(1, INTERP_TAPS):
                    total = total + taps[t] * window[c, pl.ds(shift + half * rows + t, rows), spot, :]
                parts.append(total)
            real, imag = parts
            put = slice(half * rows, (half + 1) * rows)
            moved[put, spot, :] = real * pcos + imag * psin
            low = pl.ds(pl.multiple_of(SIDE + d * deep, deep), deep)
            moved[put, low, :] = imag * pcos - real * psin
        return 0

    lax.fori_loop(0, DOPPLER_BLOCKS, block, 0)

    both = jnp.concatenate([moved[r] for r in range(BAND_BINS)], axis=1)
    first = mm3(table_ref, both, NN)
    cosine, sine = cos_ref[...], sin_ref[...]
    for r in range(BAND_BINS):
        real = first[:SIDE, r * SIDE : (r + 1) * SIDE]
        imag = first[SIDE:, r * SIDE : (r + 1) * SIDE]
        staged[slot, r, :, :SIDE] = (real * cosine - imag * sine).astype(jnp.bfloat16)
        staged[slot, r, :, SIDE:] = (imag * cosine + real * sine).astype(jnp.bfloat16)


def exchange(shifts, counts, factors, rates, replica, ftables, itable, echoes, az_count):
    ftable, cosine, sine = ftables
    rows, lines = echoes.shape[1], echoes.shape[2]
    taps = replica.shape[1]
    block_rows = COMPRESS_ROWS
    span = taps + block_rows
    width = math.gcd(256, lines)
    chunks = lines // width
    local_rows = rows // az_count
    phases = len(phase_starts(local_rows // BAND_BINS)) - 1
    vmem = pl.BlockSpec(memory_space=pltpu.VMEM)
    smem = pl.BlockSpec(memory_space=pltpu.SMEM)
    anywhere = pl.BlockSpec(memory_space=pl.ANY)
    dma = pltpu.SemaphoreType.DMA
    return pl.pallas_call(
        functools.partial(exchange_kernel, width, block_rows),
        out_shape=[
            jax.ShapeDtypeStruct((az_count, 2, local_rows + RIM_ROWS, lines), jnp.bfloat16),
            jax.ShapeDtypeStruct((local_rows, SIDE, 2 * SIDE), jnp.bfloat16),
        ],
        in_specs=[smem] * 4 + [vmem] * 5 + [anywhere],
        out_specs=[anywhere, anywhere],
        scratch_shapes=[
            pltpu.VMEM((2, rows + taps, lines), jnp.bfloat16),
            pltpu.VMEM((2, rows // 2, width), jnp.bfloat16),
            pltpu.VMEM((2, 2 * block_rows, span), jnp.bfloat16),
            pltpu.VMEM((2, az_count, 2, BAND_BINS, lines), jnp.bfloat16),
            pltpu.VMEM((BAND_BINS, 2 * SIDE, SIDE), jnp.float32),
            pltpu.VMEM((2, 2 * RIM_ROWS + BAND_BINS, SIDE, SIDE), jnp.float32),
            pltpu.VMEM((2, SIDE, SIDE), jnp.float32),
            pltpu.VMEM((2, BAND_BINS, SIDE, 2 * SIDE), jnp.bfloat16),
            dma((chunks,)),
            dma((chunks,)),
            dma((chunks,)),
            dma((max(chunks, phases),)),
            dma((phases,)),
            dma((3,)),
            dma((1,)),
            dma((2,)),
            dma((2,)),
            pltpu.SemaphoreType.REGULAR,
        ],
        compiler_params=pltpu.CompilerParams(
            vmem_limit_bytes=60 * 1024 * 1024, collective_id=0, has_side_effects=True
        ),
        cost_estimate=pl.CostEstimate(
            flops=8 * rows * span * lines + local_rows * 8 * 16 * SIDE**3,
            bytes_accessed=4 * lines * (4 * rows + taps),
            transcendentals=0,
        ),
        name="exchange",
    )(shifts.T, counts, factors.T, rates, replica, ftable, itable, cosine, sine, echoes)


def finish_kernel(table_ref, inner_ref, out_ref, image):
    rows = inner_ref.shape[0]
    both = jnp.concatenate([inner_ref[r] for r in range(rows)], axis=0)
    second = mm2(table_ref, both, NT) * (1.0 / (SIDE * SIDE))
    for r in range(rows):
        image[r] = second[:, r * SIDE : (r + 1) * SIDE]
    group = 16
    for c in range(2):
        for g in range(SIDE // group):
            piece = image[:, c * SIDE + g * group : c * SIDE + (g + 1) * group, :]
            out_ref[c, :, g * group * SIDE : (g + 1) * group * SIDE] = piece.reshape(
                rows, group * SIDE
            )


def finish(table, inner):
    local_rows = inner.shape[0]
    rows = math.gcd(32, local_rows)
    return pl.pallas_call(
        finish_kernel,
        out_shape=jax.ShapeDtypeStruct((2, local_rows, SIDE * SIDE), jnp.float32),
        grid=(local_rows // rows,),
        in_specs=[
            pl.BlockSpec(table.shape, lambda i: (0, 0, 0)),
            pl.BlockSpec((rows, SIDE, 2 * SIDE), lambda i: (i, 0, 0)),
        ],
        out_specs=pl.BlockSpec((2, rows, SIDE * SIDE), lambda i: (0, i, 0)),
        scratch_shapes=[pltpu.VMEM((rows, 2 * SIDE, SIDE), jnp.float32)],
        compiler_params=pltpu.CompilerParams(vmem_limit_bytes=VMEM),
        name="finish",
    )(table, inner)


def fill_weights(replica_ref, w_ref):
    count, span = w_ref.shape[1] // 2, w_ref.shape[2]
    taps = replica_ref[...].astype(jnp.float32)
    for c in range(2):
        padded = jnp.concatenate(
            [taps[c : c + 1], jnp.zeros((1, span - taps.shape[1]), jnp.float32)], axis=1
        )
        rows = pltpu.roll(
            jnp.broadcast_to(padded, (count, span)), 0, 1, stride=1, stride_axis=0
        )
        if c == 0:
            w_ref[0, :count] = rows.astype(jnp.bfloat16)
            w_ref[1, count:] = rows.astype(jnp.bfloat16)
        else:
            w_ref[0, count:] = (-rows).astype(jnp.bfloat16)
            w_ref[1, :count] = rows.astype(jnp.bfloat16)


def per_device(echoes, replica, shifts, tap_counts, interp_weights, fm_rates):
    az_count = lax.axis_size("az")
    forward_m, inverse_m, twist_cos, twist_sin = transform_tables()
    cosine = jnp.asarray(twist_cos, jnp.float32)
    sine = jnp.asarray(twist_sin, jnp.float32)
    forward_tables = (split_const(forward_m), cosine, sine)
    inverse_table = split_const(inverse_m)

    _, inner = exchange(
        shifts, tap_counts, interp_weights, fm_rates, replica, forward_tables, inverse_table, echoes, az_count
    )
    return finish(inverse_table, inner)


def solution(mesh):
    return jax.shard_map(
        per_device,
        mesh=mesh,
        in_specs=(P(None, "rg", "az"), P(), P(), P(), P(), P()),
        out_specs=P(None, ("rg", "az"), None),
        check_vma=False,
    )
```
